128 devices in a mesh: fx: 8 (over y, x_lo), fy: 16 (over x_hi, z, core).
Axes of the slice: x: 4 (x_hi: 2, x_lo: 2; x = x_hi * 2 + x_lo), y: 4, z: 4, core: 2. Of those that a mesh axis runs over, the one named last changes fastest.
Arguments:
- sky: bfloat16 [8192, 65536], P('fx', 'fy'), may hold values from -6 to 6
- sub_off: int32 [2, 4], replicated, may hold values from 0 to 65535
- readers: int32 [128], replicated, may hold values from 0 to 3, as said below
- vis_cells: int32 [2, 262144], P(None, ('fx', 'fy')), may hold values from 0 to 504
- row_kernel: bfloat16 [8, 262144], P(None, ('fx', 'fy')), may hold values from 0.049804688 to 1
- col_kernel: float32 [8, 262144], P(None, ('fx', 'fy')), may hold values from 0.05 to 1
Outputs:
- vis: float32 [2, 262144], P(None, ('fx', 'fy'))
The draws below stay inside these ranges and needn't reach their ends.
Inputs may be any that keep to these rules, and one draw needn't show every extreme that they name: `readers`: every subgrid is read by at least one reader.
All inputs are finite; a program needn't handle non-finite values.
Results may differ from the reference program's by a relative error of at most 0.0064.
Values may be sent and summed in bfloat16 or wider, within the bound.
A program may use at most 128 MiB of HBM per device.

```python
import math
import jax
import jax.numpy as jnp
from jax import lax

FACET = 4096
SUB = 512
K = 128
W = 8
FR = 512
NSUB = 4
NV = 2048
FACETS_X = 16
FACETS_Y = 16
SKY = 65536
READERS = 128
ROWS = 8192
VIS = 262144


def draw_readers(key, part):
    first_key, second_key, third_key = jax.random.split(key, 3)
    extra = READERS - NSUB
    first_pick = jax.random.randint(first_key, (extra,), 0, NSUB, dtype=jnp.int32)
    second_pick = jax.random.randint(second_key, (extra,), 0, NSUB, dtype=jnp.int32)
    listed = jnp.concatenate([jnp.arange(NSUB, dtype=jnp.int32), jnp.minimum(first_pick, second_pick)])
    return jax.random.permutation(third_key, listed)


def with_ends(drawn, own_key, least, largest):
    shape = drawn.shape
    place = [jax.random.randint(jax.random.fold_in(own_key, axis), (), 0, shape[axis]) for axis in range(len(shape))]
    drawn = drawn.at[tuple(place)].set(least)
    longest = shape.index(max(shape))
    place[longest] = (place[longest] + 1) % shape[longest]
    return drawn.at[tuple(place)].set(largest)


def shard_levels(rng, dims, shards, least, high):
    loudness, own = 1.0, jax.random.fold_in(rng, 6)
    for axis_at, shards_of in shards:
        heights = jnp.exp(jax.random.uniform(jax.random.fold_in(own, axis_at), (shards_of,), jnp.float32, least / len(shards), high / len(shards)))
        loudness = loudness * jnp.repeat(heights, dims[axis_at] // shards_of).reshape([-1 if axis == axis_at else 1 for axis in range(len(dims))])
    return loudness


def noise(own_key, dims, scale, limit, pieces=(), kind=jnp.bfloat16):
    loudness = shard_levels(own_key, dims, pieces, -0.22, 0.18) if pieces else 1.0
    entries = jax.random.normal(own_key, dims, jnp.float32) * scale * loudness
    return jnp.minimum(jnp.maximum(entries, -limit), limit).astype(kind)


def setup_inputs(seed: int = 0) -> dict:
    key_list = jax.random.split(jax.random.key(seed), 7)
    return {
        "sky": noise(key_list[0], (ROWS, SKY), 1.0, 6.0, ((0, 8), (1, 16))),
        "sub_off": with_ends(jax.random.randint(key_list[1], (2, NSUB), 0, SKY), jax.random.fold_in(key_list[1], 1), 0, SKY - 1).astype(jnp.int32),
        "readers": draw_readers(jax.random.fold_in(key_list[6], 71), 0),
        "vis_cells": with_ends(jax.random.randint(key_list[3], (2, VIS), 0, SUB - W + 1), jax.random.fold_in(key_list[3], 1), 0, SUB - W).astype(jnp.int32),
        "row_kernel": jnp.clip(jnp.exp(math.log(1.0) - 2.9996462 * jax.random.uniform(key_list[4], (W, VIS), jnp.float32) ** shard_levels(key_list[4], (W, VIS), ((1, 128),), -0.2, 0.2)), 0.049804688, 1.0).astype(jnp.bfloat16),
        "col_kernel": jnp.clip(jnp.exp(math.log(1.0) - 2.9957323 * jax.random.uniform(key_list[5], (W, VIS), jnp.float32) ** shard_levels(key_list[5], (W, VIS), ((1, 128),), -0.2, 0.2)), 0.05, 1.0),
    }


def phase_mod(upper, lower, sky_cells):
    return (upper % 256 * lower + upper // 256 * lower % sky_cells * 256) % sky_cells

def unit_angle(phase, sky_cells):
    return phase.astype(jnp.float32) * (2.0 * math.pi / sky_cells)

def resample_table(start, sky_cells):
    tap_index = jnp.arange(K, dtype=jnp.int32)
    grid_cells = jnp.arange(SUB, dtype=jnp.int32)
    places = (start + tap_index * (sky_cells // SUB)) % sky_cells
    forward = unit_angle(phase_mod(grid_cells[:, None], places[None, :], sky_cells), sky_cells)
    backward = -unit_angle(phase_mod(SUB // K * tap_index[None, :], places[:, None], sky_cells), sky_cells)
    wave_real, wave_imag = (jnp.cos(forward), jnp.sin(forward))
    back_real, back_imag = (jnp.cos(backward) / K, jnp.sin(backward) / K)
    highest = lax.Precision.HIGHEST
    real_part = jnp.dot(wave_real, back_real, precision=highest) - jnp.dot(wave_imag, back_imag, precision=highest)
    imag_part = jnp.dot(wave_real, back_imag, precision=highest) + jnp.dot(wave_imag, back_real, precision=highest)
    return (real_part, imag_part)

def row_stack(real_part, imag_part):
    return jnp.stack([jnp.stack([real_part, -imag_part], 1), jnp.stack([imag_part, real_part], 1)], 1).astype(jnp.bfloat16)

def col_stack(real_part, imag_part, factor):
    return jnp.stack([jnp.stack([real_part, imag_part]), jnp.stack([-imag_part, real_part])]) * factor

def strip_table(col_offsets, col_start, sky_cells):
    columns = col_start + jnp.arange(FACET, dtype=jnp.int32)
    frequency = col_offsets[:, None] + SUB // K * jnp.arange(K, dtype=jnp.int32)[None, :]
    angles = -unit_angle(phase_mod(frequency[None, :, :], columns[:, None, None], sky_cells), sky_cells)
    values_table = jnp.stack([jnp.cos(angles), jnp.sin(angles)], 2) / math.sqrt(FACET)
    return values_table.reshape(FACET, NSUB * 2 * K).astype(jnp.bfloat16)

def row_transform(row_offsets, row_start, sky_cells):
    rows_here = row_start + jnp.arange(FR, dtype=jnp.int32)
    frequency = row_offsets[:, None] + SUB // K * jnp.arange(K, dtype=jnp.int32)[None, :]
    angles = -unit_angle(phase_mod(frequency[:, :, None], rows_here[None, None, :], sky_cells), sky_cells)
    wave_real = jnp.cos(angles) / math.sqrt(FR)
    wave_imag = jnp.sin(angles) / math.sqrt(FR)
    real_rows = jnp.stack([wave_real, -wave_imag], 2)
    imag_rows = jnp.stack([wave_imag, wave_real], 2)
    return jnp.stack([real_rows, imag_rows], 1).astype(jnp.bfloat16)

def degridding(subgrid, vis_cells, row_kernel, col_kernel):
    grid_cells = jnp.arange(SUB, dtype=jnp.int32)
    row_gap = grid_cells[None, :] - vis_cells[0][:, None]
    col_gap = grid_cells[None, :] - vis_cells[1][:, None]
    row_weights = jnp.zeros(row_gap.shape, jnp.float32)
    col_weights = jnp.zeros(col_gap.shape, jnp.float32)
    for tap_index in range(row_kernel.shape[0]):
        row_weights = row_weights + jnp.where(row_gap == tap_index, row_kernel[tap_index].astype(jnp.float32)[:, None], 0.0)
        col_weights = col_weights + jnp.where(col_gap == tap_index, col_kernel[tap_index][:, None], 0.0)
    spread = jnp.dot(row_weights.astype(jnp.bfloat16), subgrid.reshape(SUB, 2 * SUB), preferred_element_type=jnp.float32)
    spread = spread.reshape(-1, 2, SUB)
    return lax.optimization_barrier(jnp.sum(spread * col_weights[:, None, :], axis=2)).T

def reference(sky, sub_off, readers, vis_cells, row_kernel, col_kernel):
    sky_cells = FACET * FACETS_Y
    row_spacing = sky_cells // FACETS_X
    factor = 1.0 / math.sqrt(FACETS_X * FACETS_Y)

    def column_turn(total, col_index):
        col_start = col_index * FACET
        values_table = strip_table(sub_off[1], col_start, sky_cells)

        def row_turn(summed, row_index):
            facet_block = lax.dynamic_slice(sky, (row_index * FR, col_start), (FR, FACET))
            strips = jnp.dot(facet_block, values_table, preferred_element_type=jnp.float32).astype(jnp.bfloat16)
            strips = strips.reshape(FR, NSUB, 2, K)
            row_start = row_index * row_spacing
            row_table = row_transform(sub_off[0], row_start, sky_cells)
            blocks = jnp.einsum('sqkpr,rspl->sqkl', row_table.astype(jnp.float32), strips.astype(jnp.float32)).astype(jnp.bfloat16)
            resampler = row_stack(*resample_table(row_start, sky_cells))
            update = jnp.einsum('mdqk,sqkl->mdsl', resampler.astype(jnp.float32), blocks.astype(jnp.float32))
            return (summed + update, None)
        summed, unused = lax.scan(row_turn, jnp.zeros((SUB, 2, NSUB, K), jnp.float32), jnp.arange(FACETS_X, dtype=jnp.int32))
        col_table = col_stack(*resample_table(col_start, sky_cells), factor)
        update = jnp.einsum('mcsl,cdnl->mdsn', summed, col_table, precision=lax.Precision.HIGHEST)
        return (total + update, None)
    total, unused = lax.scan(column_turn, jnp.zeros((SUB, 2, NSUB, SUB), jnp.float32), jnp.arange(FACETS_Y, dtype=jnp.int32))
    subgrids = total.astype(jnp.bfloat16)
    cells_by_reader = vis_cells.reshape(2, READERS, NV).transpose(1, 0, 2)
    rows_by_reader = row_kernel.reshape(W, READERS, NV).transpose(1, 0, 2)
    cols_by_reader = col_kernel.reshape(W, READERS, NV).transpose(1, 0, 2)

    def reader_turn(inputs):
        chosen, cells_here, rows_here, cols_here = inputs
        subgrid = lax.dynamic_index_in_dim(subgrids, chosen, 2, keepdims=False)
        return degridding(subgrid, cells_here, rows_here, cols_here)
    results = lax.map(reader_turn, (readers, cells_by_reader, rows_by_reader, cols_by_reader))
    return results.transpose(1, 0, 2).reshape(2, VIS)
```

```python
import functools
import math

import jax
import jax.numpy as jnp
import numpy as np
from jax import lax
from jax.experimental import pallas as pl
from jax.experimental.pallas import tpu as pltpu
from jax.sharding import PartitionSpec as P

FACET = 4096
SUB = 512
K = 128
W = 8
FR = 512
NSUB = 4
SKY = 65536
CHUNK = 512
CHUNKS = FACET // CHUNK
VTILE = 256
BF = jnp.bfloat16
F32 = jnp.float32
MESH = pl.DeviceIdType.MESH


def wave(rows, cols, period):
    turn = (np.arange(rows)[:, None] * np.arange(cols)[None, :]) % period
    angle = turn * (2.0 * math.pi / period)
    return np.cos(angle), np.sin(angle)


def small_tables():
    re, im = wave(K, K, K)
    re, im = re / K, -im / K
    cols = np.block([[re.T, im.T], [-im.T, re.T]])
    rows = np.zeros((2, 2, K, 3, 2, 64))
    for f in range(2):
        for t in range(K):
            at, cell = divmod(32 * f + t, 64)
            rows[f, 0, :, at, 0, cell] = re[t]
            rows[f, 1, :, at, 0, cell] = -im[t]
            rows[f, 0, :, at, 1, cell] = im[t]
            rows[f, 1, :, at, 1, cell] = re[t]
    qre, qim = wave(K, FR, SKY // 4)
    scale = 1.0 / math.sqrt(FR)
    return (
        jnp.asarray(cols, BF),
        jnp.asarray(rows.reshape(4 * K, 384), BF),
        jnp.asarray(qre * scale, F32),
        jnp.asarray(-qim * scale, F32),
    )


def grid_tables():
    re, im = wave(SUB, SUB, SUB)
    et = np.stack([np.concatenate([re, im], 1), np.concatenate([-im, re], 1)])
    et = et.reshape(2, 8, 64, 2 * SUB).transpose(1, 0, 2, 3).reshape(2 * SUB, 2 * SUB)
    en = np.block([[re, -im], [im, re]]) / 16.0
    return jnp.asarray(et, BF), jnp.asarray(en, BF)


def cis(phase):
    turn = phase & 0xFFFF
    quarter = (turn + 8192) >> 14
    x = (turn - (quarter << 14)).astype(F32) * (2.0 * math.pi / SKY)
    x2 = x * x
    c = 1.0 + x2 * (-0.5 + x2 * (1.0 / 24 + x2 * (-1.0 / 720 + x2 * (1.0 / 40320))))
    s = x * (1.0 + x2 * (-1.0 / 6 + x2 * (1.0 / 120 + x2 * (-1.0 / 5040 + x2 * (1.0 / 362880)))))
    odd = (quarter & 1) == 1
    cos = jnp.where(odd, s, c)
    sin = jnp.where(odd, c, s)
    cos = jnp.where(((quarter + 1) & 2) != 0, -cos, cos)
    sin = jnp.where((quarter & 2) != 0, -sin, sin)
    return cos, sin


def iota(shape, dim):
    return lax.broadcasted_iota(jnp.int32, shape, dim)


def facet_kernel(
    sky_ref, off_ref, dc_ref, dr_ref, qre_ref, qim_ref, out_ref,
    sky_v, va, vb, acc, coarse, fine, uu, sem,
):
    fx, fy = lax.axis_index("fx"), lax.axis_index("fy")

    def sky_copy(c):
        part = pl.ds(pl.multiple_of(c * CHUNK, CHUNK), CHUNK)
        return pltpu.make_async_copy(sky_ref.at[:, part], sky_v.at[:, part], sem.at[c])

    for c in range(CHUNKS):
        sky_copy(c).start()

    step, lane = iota((64, K), 0), iota((64, K), 1)
    for s in range(NSUB):
        freq = off_ref[1, s] + 4 * lane
        cos, sin = cis(freq * (64 * step + FACET * fy) + SKY // 4 * lane * fy)
        coarse[s, 0] = cos
        coarse[s, 1] = -sin
        cos, sin = cis(freq * step)
        fine[s, 0] = cos * (1.0 / 64)
        fine[s, 1] = -sin * (1.0 / 64)

    def fill(s, c, ref):
        bre, bim = fine[s, 0], fine[s, 1]
        for h in range(CHUNK // 64):
            at = pl.ds(c * (CHUNK // 64) + h, 1)
            are, aim = coarse[s, 0, at, :], coarse[s, 1, at, :]
            ref[64 * h : 64 * h + 64, 0:K] = (are * bre - aim * bim).astype(BF)
            ref[64 * h : 64 * h + 64, K : 2 * K] = (are * bim + aim * bre).astype(BF)

    def add(c, ref):
        part = pl.ds(pl.multiple_of(c * CHUNK, CHUNK), CHUNK)
        acc[...] += jnp.dot(sky_v[:, part], ref[...], preferred_element_type=F32)

    fill(0, 0, va)
    for s in range(NSUB):
        acc[...] = jnp.zeros_like(acc)

        @pl.loop(0, CHUNKS // 2)
        def _(t):
            if s == 0:
                sky_copy(2 * t).wait()
                sky_copy(2 * t + 1).wait()
            fill(s, 2 * t + 1, vb)
            add(2 * t, va)
            last = t == CHUNKS // 2 - 1
            after = jnp.where(last, min(s + 1, NSUB - 1), s)
            fill(after, jnp.where(last, 0, 2 * t + 2), va)
            add(2 * t + 1, vb)

        places = iota((1, FR), 1)
        parts = []
        for f in range(2):
            cos, sin = cis(off_ref[0, s] * (FACET * (2 * fx + f) + places))
            qre, qim = qre_ref[...], qim_ref[...]
            ure, uim = qre * cos + qim * sin, qim * cos - qre * sin
            if f == 1:
                sign = jnp.where((iota((K, 1), 0) & 1) == 1, -1.0, 1.0)
                ure, uim = ure * sign, uim * sign
            uu[0:K] = ure.astype(BF)
            uu[K : 2 * K] = uim.astype(BF)
            strips = acc[FR * f : FR * (f + 1)].astype(BF)
            mixed = jnp.dot(uu[...], strips, preferred_element_type=F32)
            bre = mixed[:K, :K] - mixed[K:, K:]
            bim = mixed[:K, K:] + mixed[K:, :K]
            block = jnp.concatenate([bre, bim], 1).astype(BF)
            image = jnp.dot(block, dc_ref[...], preferred_element_type=F32)
            parts += [image[:, :K].T.astype(BF), image[:, K:].T.astype(BF)]
        window = jnp.dot(
            jnp.concatenate(parts, 1), dr_ref[...], preferred_element_type=F32
        ).astype(BF)
        for di in range(3):
            for dj in range(4):
                out_ref[di * 4 + dj, s] = window[32 * dj : 32 * dj + 32, 128 * di : 128 * di + 128]


def facets(sky, sub_off):
    any_space = pl.BlockSpec(memory_space=pl.ANY)
    vmem = pl.BlockSpec(memory_space=pltpu.VMEM)
    return pl.pallas_call(
        facet_kernel,
        out_shape=jax.ShapeDtypeStruct((12, NSUB, 32, 128), BF),
        in_specs=[any_space, pl.BlockSpec(memory_space=pltpu.SMEM), vmem, vmem, vmem, vmem],
        out_specs=vmem,
        scratch_shapes=[
            pltpu.VMEM((2 * FR, FACET), BF),
            pltpu.VMEM((CHUNK, 2 * K), BF),
            pltpu.VMEM((CHUNK, 2 * K), BF),
            pltpu.VMEM((2 * FR, 2 * K), F32),
            pltpu.VMEM((NSUB, 2, 64, K), F32),
            pltpu.VMEM((NSUB, 2, 64, K), F32),
            pltpu.VMEM((2 * K, FR), BF),
            pltpu.SemaphoreType.DMA((CHUNKS,)),
        ],
        compiler_params=pltpu.CompilerParams(vmem_limit_bytes=40 * 2**20),
    )(sky, sub_off, *small_tables())


def exchange_kernel(
    pieces_ref, readers_ref, out_ref,
    halo, plane, outbox, fin, halo_sems, plane_sems, last_sems,
):
    fx, fy = lax.axis_index("fx"), lax.axis_index("fy")
    y, core, z = fx // 2, fy % 2, (fy // 2) % 4
    x = 2 * (fy // 8) + fx % 2
    first = core == 0

    def device(x, y, z, core):
        return (2 * y + x % 2, (x // 2) * 8 + 2 * z + core)

    def axis_of(core):
        return jnp.where(core == 0, x, z)

    def halo_peer(k, sign):
        return ((fx + sign * (k // 4) + 8) % 8, (fy + sign * (k % 4) + 16) % 16)

    def plane_peer(k, sign):
        far = (jnp.where(first, z, x) + sign * (k // 4) + 4) % 4
        yy = (y + sign * (k % 4) + 4) % 4
        return device(jnp.where(first, x, far), yy, jnp.where(first, far, z), core), far * 4 + yy

    def last_peer(k, sign):
        other = (core + k % 2) % 2
        mover = core if sign == 1 else other
        place = (axis_of(mover) + sign * (k // 2) + 4) % 4
        xx, zz = jnp.where(mover == 0, place, x), jnp.where(mover == 0, z, place)
        slot = mover * 4 + (axis_of(mover) if sign == 1 else place)
        return device(xx, y, zz, other), slot

    barrier = pltpu.get_barrier_semaphore()
    for k in range(1, 12):
        pl.semaphore_signal(barrier, inc=1, device_id=halo_peer(k, -1), device_id_type=MESH)
    for k in range(1, 16):
        pl.semaphore_signal(barrier, inc=1, device_id=plane_peer(k, -1)[0], device_id_type=MESH)
    for k in range(1, 8):
        pl.semaphore_signal(barrier, inc=1, device_id=last_peer(k, -1)[0], device_id_type=MESH)
    pl.semaphore_wait(barrier, 33)

    def halo_copy(k):
        return pltpu.make_async_remote_copy(
            src_ref=pieces_ref.at[k], dst_ref=halo.at[k],
            send_sem=halo_sems.at[0, k], recv_sem=halo_sems.at[1, k],
            device_id=halo_peer(k, 1), device_id_type=MESH,
        )

    own = jnp.where(first, z, x) * 4 + y

    def plane_copy(k, slot):
        return pltpu.make_async_remote_copy(
            src_ref=plane.at[own], dst_ref=plane.at[slot],
            send_sem=plane_sems.at[0, k], recv_sem=plane_sems.at[1, k],
            device_id=plane_peer(k, 1)[0], device_id_type=MESH,
        )

    def last_copy(k, slot):
        return pltpu.make_async_remote_copy(
            src_ref=outbox.at[k], dst_ref=fin.at[slot],
            send_sem=last_sems.at[0, k], recv_sem=last_sems.at[1, k],
            device_id=last_peer(k, 1)[0], device_id_type=MESH,
        )

    for k in range(1, 12):
        halo_copy(k).start()
    total = pieces_ref[0].astype(F32)
    for k in range(1, 12):
        halo_copy(k).wait_recv()
        total = total + halo[k].astype(F32)
    plane[own] = total.astype(BF)
    for k in range(1, 16):
        plane_copy(k, own).start()
    for k in range(1, 16):
        plane_copy(k, plane_peer(k, -1)[1]).wait_recv()
    mine = core * 4 + axis_of(core)
    for k in range(1, 8):
        peer = last_peer(k, 1)[0]
        outbox[k] = plane[:, readers_ref[peer[0] * 16 + peer[1]]]
        last_copy(k, mine).start()
    fin[mine] = plane[:, readers_ref[fx * 16 + fy]]
    for k in range(1, 8):
        last_copy(k, last_peer(k, -1)[1]).wait_recv()
    for k in range(1, 12):
        halo_copy(k).wait_send()
    for k in range(1, 16):
        plane_copy(k, own).wait_send()
    for k in range(1, 8):
        last_copy(k, mine).wait_send()
    out_ref[...] = fin[...]


def exchange(pieces, readers):
    vmem = pl.BlockSpec(memory_space=pltpu.VMEM)
    return pl.pallas_call(
        exchange_kernel,
        out_shape=jax.ShapeDtypeStruct((8, 16, 32, 128), BF),
        in_specs=[vmem, pl.BlockSpec(memory_space=pltpu.SMEM)],
        out_specs=vmem,
        scratch_shapes=[
            pltpu.VMEM((12, NSUB, 32, 128), BF),
            pltpu.VMEM((16, NSUB, 32, 128), BF),
            pltpu.VMEM((8, 16, 32, 128), BF),
            pltpu.VMEM((8, 16, 32, 128), BF),
            pltpu.SemaphoreType.DMA((2, 12)),
            pltpu.SemaphoreType.DMA((2, 16)),
            pltpu.SemaphoreType.DMA((2, 8)),
        ],
        compiler_params=pltpu.CompilerParams(
            collective_id=0, has_side_effects=True, vmem_limit_bytes=32 * 2**20
        ),
    )(pieces, readers)


def place_of(i, j):
    x, y, z, core = 2 * (j // 8) + i % 2, i // 2, (j // 2) % 4, j % 2
    return (4 + z, x * 4 + y) if core else (x, z * 4 + y)


def turned(kernel, start):
    first = start & 7
    row = iota(kernel.shape, 0)
    laid = kernel
    for r in range(1, 8):
        laid = jnp.where(first == r, jnp.roll(kernel, r, 0), laid)
    return laid, (start >> 3) + jnp.where(row < first, 1, 0)


def degrid_kernel(fin_ref, cells_ref, rows_ref, cols_ref, et_ref, en_ref, out_ref, yy, grid_t):
    for j in range(0, 16, 2):
        lhs = []
        for i in range(8):
            at = [place_of(i, j + d) for d in range(2)]
            lhs.append(jnp.concatenate([fin_ref[a, b] for a, b in at], 0))
        done = jnp.dot(jnp.concatenate(lhs, 1), et_ref[...], preferred_element_type=F32).astype(BF)
        yy[32 * j : 32 * j + 64] = done[:, :SUB]
        yy[SUB + 32 * j : SUB + 32 * j + 64] = done[:, SUB:]

    @pl.loop(0, 8)
    def _(h):
        part = pl.ds(pl.multiple_of(h * 128, 128), 128)
        grid_t[part] = jnp.dot(en_ref[part], yy[...], preferred_element_type=F32).astype(BF)

    @pl.loop(0, cells_ref.shape[1] // VTILE)
    def _(t):
        at = pl.ds(pl.multiple_of(t * VTILE, VTILE), VTILE)
        taps, block = turned(rows_ref[:, at].astype(F32), cells_ref[0:1, at])
        across = iota((SUB // 8, 8, VTILE), 0)
        spread = jnp.where(across == block[None], taps[None], 0.0).reshape(SUB, VTILE).astype(BF)
        taps, block = turned(cols_ref[:, at], cells_ref[1:2, at])
        sums = [jnp.zeros((8, VTILE), F32), jnp.zeros((8, VTILE), F32)]
        for c in range(4):
            here = (iota((16, 8, VTILE), 0) + 16 * c) == block[None]
            for p in range(2):
                part = grid_t[SUB * p + 128 * c : SUB * p + 128 * c + 128]
                values = jnp.dot(part, spread, preferred_element_type=F32)
                values = values.reshape(16, 8, VTILE)
                sums[p] = sums[p] + jnp.sum(jnp.where(here, values, 0.0), axis=0)
        for p in range(2):
            out_ref[p : p + 1, at] = jnp.sum(sums[p] * taps, axis=0, keepdims=True)


def degrid(fin, vis_cells, row_kernel, col_kernel):
    vmem = pl.BlockSpec(memory_space=pltpu.VMEM)
    return pl.pallas_call(
        degrid_kernel,
        out_shape=jax.ShapeDtypeStruct((2, vis_cells.shape[1]), F32),
        in_specs=[vmem] * 6,
        out_specs=vmem,
        scratch_shapes=[
            pltpu.VMEM((2 * SUB, SUB), BF),
            pltpu.VMEM((2 * SUB, SUB), BF),
        ],
        compiler_params=pltpu.CompilerParams(vmem_limit_bytes=32 * 2**20),
    )(fin, vis_cells, row_kernel, col_kernel, *grid_tables())


def local(sky, sub_off, readers, vis_cells, row_kernel, col_kernel):
    pieces = facets(sky, sub_off)
    fin = exchange(pieces, readers)
    return degrid(fin, vis_cells, row_kernel, col_kernel)


def solution(mesh):
    return jax.shard_map(
        local,
        mesh=mesh,
        in_specs=(
            P("fx", "fy"),
            P(),
            P(),
            P(None, ("fx", "fy")),
            P(None, ("fx", "fy")),
            P(None, ("fx", "fy")),
        ),
        out_specs=P(None, ("fx", "fy")),
        check_vma=False,
    )
```

```python
import math

import jax
import jax.numpy as jnp
import numpy as np
from jax import lax
from jax.experimental import pallas as pl
from jax.experimental.pallas import tpu as pltpu
from jax.sharding import PartitionSpec as P

FACET = 4096
SUB = 512
K = 128
W = 8
FR = 512
NSUB = 4
SKY = 65536
CHUNK = 512
CHUNKS = FACET // CHUNK
VTILE = 256
BF = jnp.bfloat16
F32 = jnp.float32
MESH = pl.DeviceIdType.MESH


def wave(rows, cols, period):
    turn = (np.arange(rows)[:, None] * np.arange(cols)[None, :]) % period
    angle = turn * (2.0 * math.pi / period)
    return np.cos(angle), np.sin(angle)


def small_tables():
    re, im = wave(K, K, K)
    re, im = re / K, -im / K
    cols = np.block([[re.T, im.T], [-im.T, re.T]])
    rows = np.zeros((2, 2, K, 3, 2, 64))
    for f in range(2):
        for t in range(K):
            at, cell = divmod(32 * f + t, 64)
            rows[f, 0, :, at, 0, cell] = re[t]
            rows[f, 1, :, at, 0, cell] = -im[t]
            rows[f, 0, :, at, 1, cell] = im[t]
            rows[f, 1, :, at, 1, cell] = re[t]
    qre, qim = wave(K, FR, SKY // 4)
    scale = 1.0 / math.sqrt(FR)
    return (
        jnp.asarray(cols, BF),
        jnp.asarray(rows.reshape(4 * K, 384), BF),
        jnp.asarray(qre * scale, F32),
        jnp.asarray(-qim * scale, F32),
    )


def grid_tables():
    re, im = wave(SUB, SUB, SUB)
    et = np.stack([np.concatenate([re, im], 1), np.concatenate([-im, re], 1)])
    et = et.reshape(2, 8, 64, 2 * SUB).transpose(1, 0, 2, 3).reshape(2 * SUB, 2 * SUB)
    en = np.block([[re, -im], [im, re]]) / 16.0
    return jnp.asarray(et, BF), jnp.asarray(en, BF)


def cis(phase):
    turn = phase & 0xFFFF
    quarter = (turn + 8192) >> 14
    x = (turn - (quarter << 14)).astype(F32) * (2.0 * math.pi / SKY)
    x2 = x * x
    c = 1.0 + x2 * (-0.5 + x2 * (1.0 / 24 + x2 * (-1.0 / 720 + x2 * (1.0 / 40320))))
    s = x * (1.0 + x2 * (-1.0 / 6 + x2 * (1.0 / 120 + x2 * (-1.0 / 5040 + x2 * (1.0 / 362880)))))
    odd = (quarter & 1) == 1
    cos = jnp.where(odd, s, c)
    sin = jnp.where(odd, c, s)
    cos = jnp.where(((quarter + 1) & 2) != 0, -cos, cos)
    sin = jnp.where((quarter & 2) != 0, -sin, sin)
    return cos, sin


def iota(shape, dim):
    return lax.broadcasted_iota(jnp.int32, shape, dim)


def turned(kernel, start):
    first = start & 7
    row = iota(kernel.shape, 0)
    laid = kernel
    for r in range(1, 8):
        laid = jnp.where(first == r, jnp.roll(kernel, r, 0), laid)
    return laid, (start >> 3) + jnp.where(row < first, 1, 0)


def place_of(i, j):
    j = (j + 15) % 16
    x, y, z, core = 2 * (j // 8) + i % 2, i // 2, (j // 2) % 4, j % 2
    return (4 + z, x * 4 + y) if core else (x, z * 4 + y)


def kernel(
    sky_ref, off_ref, readers_ref, cells_ref, rows_ref, cols_ref,
    dc_ref, dr_ref, qre_ref, qim_ref, et_ref, en_ref, out_ref,
    sky_v, va, vb, acc, coarse, fine, uu, pieces, halo, plane, outbox, fin,
    lhs, yy, grid_t, spread, taps, blocks, et, en, dc, dr, qre_v, qim_v, cells, rows, cols,
    sky_sems, load_sems, halo_sems, plane_sems, last_sems,
):
    fx, fy = lax.axis_index("fx"), lax.axis_index("fy")
    y, core, z = fx // 2, fy % 2, (fy // 2) % 4
    x = 2 * (fy // 8) + fx % 2
    first = core == 0

    def sky_copy(c):
        part = pl.ds(c * CHUNK, CHUNK)
        return pltpu.make_async_copy(sky_ref.at[:, part], sky_v.at[:, part], sky_sems.at[c])

    moves = [
        (dc_ref, dc), (dr_ref, dr), (qre_ref, qre_v), (qim_ref, qim_v),
        (cells_ref, cells), (rows_ref, rows), (cols_ref, cols), (et_ref, et), (en_ref, en),
    ]
    loads = [
        pltpu.make_async_copy(src, dst, load_sems.at[n]) for n, (src, dst) in enumerate(moves)
    ]
    for c in range(CHUNKS):
        sky_copy(c).start()
    for load in loads:
        load.start()

    def device(x, y, z, core):
        return (2 * y + x % 2, (x // 2) * 8 + 2 * z + core)

    def axis_of(core):
        return jnp.where(core == 0, x, z)

    def halo_peer(k, sign):
        return ((fx + sign * (k // 4) + 8) % 8, (fy + sign * (k % 4 - 1) + 16) % 16)

    def plane_peer(k, sign):
        far = (jnp.where(first, z, x) + sign * (k // 4) + 4) % 4
        yy = (y + sign * (k % 4) + 4) % 4
        return device(jnp.where(first, x, far), yy, jnp.where(first, far, z), core), far * 4 + yy

    def last_peer(k, sign):
        other = (core + k % 2) % 2
        mover = core if sign == 1 else other
        place = (axis_of(mover) + sign * (k // 2) + 4) % 4
        xx, zz = jnp.where(mover == 0, place, x), jnp.where(mover == 0, z, place)
        slot = mover * 4 + (axis_of(mover) if sign == 1 else place)
        return device(xx, y, zz, other), slot

    halo_ks = [k for k in range(12) if k != 1]
    barrier = pltpu.get_barrier_semaphore()
    for k in halo_ks:
        pl.semaphore_signal(barrier, inc=1, device_id=halo_peer(k, -1), device_id_type=MESH)
    for k in range(1, 16):
        pl.semaphore_signal(barrier, inc=1, device_id=plane_peer(k, -1)[0], device_id_type=MESH)
    for k in range(1, 8):
        pl.semaphore_signal(barrier, inc=1, device_id=last_peer(k, -1)[0], device_id_type=MESH)

    own = jnp.where(first, z, x) * 4 + y
    mine = core * 4 + axis_of(core)

    def halo_copy(s, k):
        return pltpu.make_async_remote_copy(
            src_ref=pieces.at[s, k], dst_ref=halo.at[s, k],
            send_sem=halo_sems.at[0, s, k], recv_sem=halo_sems.at[1, s, k],
            device_id=halo_peer(k, 1), device_id_type=MESH,
        )

    def plane_copy(s, k, slot):
        return pltpu.make_async_remote_copy(
            src_ref=plane.at[s, own], dst_ref=plane.at[s, slot],
            send_sem=plane_sems.at[0, s, k], recv_sem=plane_sems.at[1, s, k],
            device_id=plane_peer(k, 1)[0], device_id_type=MESH,
        )

    def last_copy(k, slot):
        return pltpu.make_async_remote_copy(
            src_ref=outbox.at[k], dst_ref=fin.at[slot],
            send_sem=last_sems.at[0, k], recv_sem=last_sems.at[1, k],
            device_id=last_peer(k, 1)[0], device_id_type=MESH,
        )

    step, lane = iota((64, K), 0), iota((64, K), 1)
    for s in range(NSUB):
        freq = off_ref[1, s] + 4 * lane
        cos, sin = cis(freq * (64 * step + FACET * fy) + SKY // 4 * lane * fy)
        coarse[s, 0] = cos
        coarse[s, 1] = -sin
        cos, sin = cis(freq * step)
        fine[s, 0] = cos * (1.0 / 64)
        fine[s, 1] = -sin * (1.0 / 64)

    def fill(s, h, ref):
        bre, bim = fine[s, 0], fine[s, 1]
        are, aim = coarse[s, 0, pl.ds(h, 1), :], coarse[s, 1, pl.ds(h, 1), :]
        at = pl.ds(pl.multiple_of(h * 64, 64), 64)
        ref[at, 0:K] = (are * bre - aim * bim).astype(BF)
        ref[at, K : 2 * K] = (are * bim + aim * bre).astype(BF)

    def strips_of(s, table, after):
        if s == 0:
            for c in range(0, CHUNKS, 2):
                sky_copy(c).wait()
                sky_copy(c + 1).wait()
                part = slice(c * CHUNK, (c + 2) * CHUNK)
                added = jnp.dot(sky_v[:, part], table[part], preferred_element_type=F32)
                acc[...] = added if c == 0 else acc[...] + added
                for h in range(8 * c, 8 * c + 16):
                    fill(s + 1, h, after)
        else:

            @pl.loop(0, 2)
            def _(t):
                part = pl.ds(pl.multiple_of(t * FR, FR), FR)
                acc[part] = jnp.dot(sky_v[part, :], table[...], preferred_element_type=F32)
                if s + 1 < NSUB:
                    for h in range(32):
                        fill(s + 1, 32 * t + h, after)

    def window_of(s):
        places = iota((1, FR), 1)
        parts = []
        for f in range(2):
            cos, sin = cis(off_ref[0, s] * (FACET * (2 * fx + f) + places))
            qre, qim = qre_v[...], qim_v[...]
            ure, uim = qre * cos + qim * sin, qim * cos - qre * sin
            if f == 1:
                sign = jnp.where((iota((K, 1), 0) & 1) == 1, -1.0, 1.0)
                ure, uim = ure * sign, uim * sign
            uu[0:K] = ure.astype(BF)
            uu[K : 2 * K] = uim.astype(BF)
            strips = acc[FR * f : FR * (f + 1)].astype(BF)
            mixed = jnp.dot(uu[...], strips, preferred_element_type=F32)
            bre = mixed[:K, :K] - mixed[K:, K:]
            bim = mixed[:K, K:] + mixed[K:, :K]
            block = jnp.concatenate([bre, bim], 1).astype(BF)
            image = jnp.dot(block, dc[...], preferred_element_type=F32)
            parts += [image[:, :K].T.astype(BF), image[:, K:].T.astype(BF)]
        window = jnp.dot(jnp.concatenate(parts, 1), dr[...], preferred_element_type=F32)
        window = window.astype(BF)
        for di in range(3):
            for dj in range(4):
                pieces[s, di * 4 + dj] = window[32 * dj : 32 * dj + 32, 128 * di : 128 * di + 128]

    def sum_halo(s):
        total = pieces[s, 1].astype(F32)
        for k in halo_ks:
            halo_copy(s, k).wait_recv()
            total = total + halo[s, k].astype(F32)
        plane[s, own] = total.astype(BF)
        for k in range(1, 16):
            plane_copy(s, k, own).start()

    @pl.loop(0, 64)
    def _(h):
        fill(0, h, va)

    for s in range(NSUB):
        table, after = (va, vb) if s % 2 == 0 else (vb, va)
        strips_of(s, table, after)
        if s == 0:
            for load in loads[:4]:
                load.wait()
        window_of(s)
        if s == 0:
            pl.semaphore_wait(barrier, 33)
        for k in halo_ks:
            halo_copy(s, k).start()
        if s >= 2:
            sum_halo(s - 2)

    for load in loads[4:]:
        load.wait()
    tiles = cells.shape[1] // VTILE

    @pl.loop(0, tiles)
    def _(t):
        at = pl.ds(pl.multiple_of(t * VTILE, VTILE), VTILE)
        laid, block = turned(rows[:, at].astype(F32), cells[0:1, at])
        across = iota((SUB // 8, 8, VTILE), 0)
        weights = jnp.where(across == block[None], laid[None], 0.0)
        spread[:, at] = weights.reshape(SUB, VTILE).astype(BF)
        laid, block = turned(cols[:, at], cells[1:2, at])
        taps[:, at] = laid
        blocks[:, at] = block

    sum_halo(2)
    sum_halo(3)
    for s in range(NSUB):
        for k in range(1, 16):
            plane_copy(s, k, plane_peer(k, -1)[1]).wait_recv()
    for k in range(1, 8):
        peer = last_peer(k, 1)[0]
        outbox[k] = plane[readers_ref[peer[0] * 16 + peer[1]]]
        last_copy(k, mine).start()
    fin[mine] = plane[readers_ref[fx * 16 + fy]]
    for k in range(1, 8):
        last_copy(k, last_peer(k, -1)[1]).wait_recv()

    for i in range(8):
        for j in range(16):
            a, b = place_of(i, j)
            lhs[32 * j : 32 * j + 32, 128 * i : 128 * i + 128] = fin[a, b]
    for h in range(2):
        at = slice(SUB * h, SUB * h + SUB)
        yy[at] = jnp.dot(lhs[...], et[:, at], preferred_element_type=F32).astype(BF)
    for h in range(2):
        at = slice(SUB * h, SUB * h + SUB)
        grid_t[at] = jnp.dot(en[at], yy[...], preferred_element_type=F32).astype(BF)

    @pl.loop(0, tiles)
    def _(t):
        at = pl.ds(pl.multiple_of(t * VTILE, VTILE), VTILE)
        block = blocks[:, at]
        sums = [jnp.zeros((8, VTILE), F32), jnp.zeros((8, VTILE), F32)]
        for c in range(4):
            here = (iota((16, 8, VTILE), 0) + 16 * c) == block[None]
            for p in range(2):
                part = grid_t[SUB * p + 128 * c : SUB * p + 128 * c + 128]
                values = jnp.dot(part, spread[:, at], preferred_element_type=F32)
                values = values.reshape(16, 8, VTILE)
                sums[p] = sums[p] + jnp.sum(jnp.where(here, values, 0.0), axis=0)
        for p in range(2):
            out_ref[p : p + 1, at] = jnp.sum(sums[p] * taps[:, at], axis=0, keepdims=True)

    for s in range(NSUB):
        for k in halo_ks:
            halo_copy(s, k).wait_send()
        for k in range(1, 16):
            plane_copy(s, k, own).wait_send()
    for k in range(1, 8):
        last_copy(k, mine).wait_send()


def local(sky, sub_off, readers, vis_cells, row_kernel, col_kernel):
    hbm = pl.BlockSpec(memory_space=pltpu.HBM)
    smem = pl.BlockSpec(memory_space=pltpu.SMEM)
    count = vis_cells.shape[1]
    return pl.pallas_call(
        kernel,
        out_shape=jax.ShapeDtypeStruct((2, count), F32),
        in_specs=[hbm, smem, smem] + [hbm] * 9,
        out_specs=pl.BlockSpec(memory_space=pltpu.VMEM),
        scratch_shapes=[
            pltpu.VMEM((2 * FR, FACET), BF),
            pltpu.VMEM((FACET, 2 * K), BF),
            pltpu.VMEM((FACET, 2 * K), BF),
            pltpu.VMEM((2 * FR, 2 * K), F32),
            pltpu.VMEM((NSUB, 2, 64, K), F32),
            pltpu.VMEM((NSUB, 2, 64, K), F32),
            pltpu.VMEM((2 * K, FR), BF),
            pltpu.VMEM((NSUB, 12, 32, 128), BF),
            pltpu.VMEM((NSUB, 12, 32, 128), BF),
            pltpu.VMEM((NSUB, 16, 32, 128), BF),
            pltpu.VMEM((8, 16, 32, 128), BF),
            pltpu.VMEM((8, 16, 32, 128), BF),
            pltpu.VMEM((SUB, 2 * SUB), BF),
            pltpu.VMEM((2 * SUB, SUB), BF),
            pltpu.VMEM((2 * SUB, SUB), BF),
            pltpu.VMEM((SUB, count), BF),
            pltpu.VMEM((8, count), F32),
            pltpu.VMEM((8, count), jnp.int32),
            pltpu.VMEM((2 * SUB, 2 * SUB), BF),
            pltpu.VMEM((2 * SUB, 2 * SUB), BF),
            pltpu.VMEM((2 * K, 2 * K), BF),
            pltpu.VMEM((4 * K, 384), BF),
            pltpu.VMEM((K, FR), F32),
            pltpu.VMEM((K, FR), F32),
            pltpu.VMEM((2, count), jnp.int32),
            pltpu.VMEM((8, count), BF),
            pltpu.VMEM((8, count), F32),
            pltpu.SemaphoreType.DMA((CHUNKS,)),
            pltpu.SemaphoreType.DMA((9,)),
            pltpu.SemaphoreType.DMA((2, NSUB, 12)),
            pltpu.SemaphoreType.DMA((2, NSUB, 16)),
            pltpu.SemaphoreType.DMA((2, 8)),
        ],
        compiler_params=pltpu.CompilerParams(
            collective_id=0, has_side_effects=True, vmem_limit_bytes=56 * 2**20
        ),
    )(sky, sub_off, readers, vis_cells, row_kernel, col_kernel, *small_tables(), *grid_tables())


def solution(mesh):
    return jax.shard_map(
        local,
        mesh=mesh,
        in_specs=(
            P("fx", "fy"),
            P(),
            P(),
            P(None, ("fx", "fy")),
            P(None, ("fx", "fy")),
            P(None, ("fx", "fy")),
        ),
        out_specs=P(None, ("fx", "fy")),
        check_vma=False,
    )
```

```python
import math

import jax
import jax.numpy as jnp
import numpy as np
from jax import lax
from jax.experimental import pallas as pl
from jax.experimental.pallas import tpu as pltpu
from jax.sharding import PartitionSpec as P

FACET = 4096
SUB = 512
K = 128
W = 8
FR = 512
NSUB = 4
SKY = 65536
CHUNK = 256
CHUNKS = 2 * FR // CHUNK
VTILE = 256
BF = jnp.bfloat16
F32 = jnp.float32
MESH = pl.DeviceIdType.MESH


def wave(rows, cols, period):
    turn = (np.arange(rows)[:, None] * np.arange(cols)[None, :]) % period
    angle = turn * (2.0 * math.pi / period)
    return np.cos(angle), np.sin(angle)


def small_tables():
    re, im = wave(K, K, K)
    re, im = re / K, -im / K
    cols = np.block([[re.T, im.T], [-im.T, re.T]])
    rows = np.zeros((2, 2, K, 3, 2, 64))
    for f in range(2):
        for t in range(K):
            at, cell = divmod(32 * f + t, 64)
            rows[f, 0, :, at, 0, cell] = re[t]
            rows[f, 1, :, at, 0, cell] = -im[t]
            rows[f, 0, :, at, 1, cell] = im[t]
            rows[f, 1, :, at, 1, cell] = re[t]
    qre, qim = wave(K, FR, SKY // 4)
    scale = 1.0 / math.sqrt(FR)
    return (
        jnp.asarray(cols, BF),
        jnp.asarray(rows.reshape(4 * K, 384), BF),
        jnp.asarray(qre * scale, F32),
        jnp.asarray(-qim * scale, F32),
    )


def grid_tables():
    re, im = wave(SUB, SUB, SUB)
    et = np.stack([np.concatenate([re, im], 1), np.concatenate([-im, re], 1)])
    et = et.reshape(2, 8, 64, 2 * SUB).transpose(1, 0, 2, 3).reshape(2 * SUB, 2 * SUB)
    en = np.block([[re, -im], [im, re]]) / 16.0
    return jnp.asarray(et, BF), jnp.asarray(en, BF)


def cis(phase):
    turn = phase & 0xFFFF
    quarter = (turn + 8192) >> 14
    x = (turn - (quarter << 14)).astype(F32) * (2.0 * math.pi / SKY)
    x2 = x * x
    c = 1.0 + x2 * (-0.5 + x2 * (1.0 / 24 + x2 * (-1.0 / 720 + x2 * (1.0 / 40320))))
    s = x * (1.0 + x2 * (-1.0 / 6 + x2 * (1.0 / 120 + x2 * (-1.0 / 5040 + x2 * (1.0 / 362880)))))
    odd = (quarter & 1) == 1
    cos = jnp.where(odd, s, c)
    sin = jnp.where(odd, c, s)
    cos = jnp.where(((quarter + 1) & 2) != 0, -cos, cos)
    sin = jnp.where((quarter & 2) != 0, -sin, sin)
    return cos, sin


def iota(shape, dim):
    return lax.broadcasted_iota(jnp.int32, shape, dim)


def turned(kernel, start):
    first = start & 7
    row = iota(kernel.shape, 0)
    laid = kernel
    for r in range(1, 8):
        laid = jnp.where(first == r, jnp.roll(kernel, r, 0), laid)
    return laid, (start >> 3) + jnp.where(row < first, 1, 0)


def place_of(i, j):
    j = (j + 15) % 16
    x, y, z, core = 2 * (j // 8) + i % 2, i // 2, (j // 2) % 4, j % 2
    return (4 + z, x * 4 + y) if core else (x, z * 4 + y)


def kernel(
    sky_ref, off_ref, readers_ref, cells_ref, rows_ref, cols_ref,
    dc_ref, dr_ref, qre_ref, qim_ref, et_ref, en_ref, out_ref,
    sky_v, va, vb, acc, coarse, fine, images, pieces, halo, plane, outbox, fin,
    lhs, yy, grid_t, spread, taps, blocks, et, en, dc, dr, qre_v, qim_v, cells, rows, cols,
    sky_sems, load_sems, send_sems, halo_sems, plane_sems, last_sems,
):
    fx, fy = lax.axis_index("fx"), lax.axis_index("fy")
    y, core, z = fx // 2, fy % 2, (fy // 2) % 4
    x = 2 * (fy // 8) + fx % 2
    first = core == 0

    def sky_copy(c):
        part = pl.ds(c * CHUNK, CHUNK)
        return pltpu.make_async_copy(sky_ref.at[part], sky_v.at[part], sky_sems.at[c])

    moves = [
        (dc_ref, dc), (dr_ref, dr), (qre_ref, qre_v), (qim_ref, qim_v),
        (cells_ref, cells), (rows_ref, rows), (cols_ref, cols), (et_ref, et), (en_ref, en),
    ]
    loads = [
        pltpu.make_async_copy(src, dst, load_sems.at[n]) for n, (src, dst) in enumerate(moves)
    ]
    for c in range(CHUNKS):
        sky_copy(c).start()
    for load in loads:
        load.start()

    def device(x, y, z, core):
        return (2 * y + x % 2, (x // 2) * 8 + 2 * z + core)

    def axis_of(core):
        return jnp.where(core == 0, x, z)

    def halo_peer(k, sign):
        return ((fx + sign * (k // 4) + 8) % 8, (fy + sign * (k % 4 - 1) + 16) % 16)

    def plane_peer(k, sign):
        far = (jnp.where(first, z, x) + sign * (k // 4) + 4) % 4
        yy = (y + sign * (k % 4) + 4) % 4
        return device(jnp.where(first, x, far), yy, jnp.where(first, far, z), core), far * 4 + yy

    def last_peer(k, sign):
        other = (core + k % 2) % 2
        mover = core if sign == 1 else other
        place = (axis_of(mover) + sign * (k // 2) + 4) % 4
        xx, zz = jnp.where(mover == 0, place, x), jnp.where(mover == 0, z, place)
        slot = mover * 4 + (axis_of(mover) if sign == 1 else place)
        return device(xx, y, zz, other), slot

    halo_ks = [k for k in range(12) if k != 1]
    halo_to = [halo_peer(k, 1) for k in halo_ks]
    plane_to = [plane_peer(k, 1)[0] for k in range(1, 16)]
    last_to = [last_peer(k, 1)[0] for k in range(1, 8)]
    barrier = pltpu.get_barrier_semaphore()
    for k in halo_ks:
        pl.semaphore_signal(barrier, inc=1, device_id=halo_peer(k, -1), device_id_type=MESH)
    for k in range(1, 16):
        pl.semaphore_signal(barrier, inc=1, device_id=plane_peer(k, -1)[0], device_id_type=MESH)
    for k in range(1, 8):
        pl.semaphore_signal(barrier, inc=1, device_id=last_peer(k, -1)[0], device_id_type=MESH)

    own = jnp.where(first, z, x) * 4 + y
    mine = core * 4 + axis_of(core)

    def halo_copy(s, k):
        return pltpu.make_async_remote_copy(
            src_ref=pieces.at[s, k], dst_ref=halo.at[s, k],
            send_sem=send_sems.at[0], recv_sem=halo_sems.at[s],
            device_id=halo_to[k], device_id_type=MESH,
        )

    def plane_copy(s, k):
        return pltpu.make_async_remote_copy(
            src_ref=plane.at[s, own], dst_ref=plane.at[s, own],
            send_sem=send_sems.at[1], recv_sem=plane_sems.at[s],
            device_id=plane_to[k], device_id_type=MESH,
        )

    def last_copy(k, slot):
        return pltpu.make_async_remote_copy(
            src_ref=outbox.at[k], dst_ref=fin.at[slot],
            send_sem=send_sems.at[2], recv_sem=last_sems.at[k],
            device_id=last_to[k], device_id_type=MESH,
        )

    def wait_for(sem, ref):
        pltpu.make_async_copy(ref, ref, sem).wait()

    step, lane = iota((64, K), 0), iota((64, K), 1)
    for s in range(NSUB):
        freq = off_ref[1, s] + 4 * lane
        cos, sin = cis(freq * (64 * step + FACET * fy) + SKY // 4 * lane * fy)
        coarse[s, 0] = cos
        coarse[s, 1] = -sin
        cos, sin = cis(freq * step)
        fine[s, 0] = cos * (1.0 / 64)
        fine[s, 1] = -sin * (1.0 / 64)

    def fill(s, h, ref):
        bre, bim = fine[s, 0], fine[s, 1]
        are, aim = coarse[s, 0, pl.ds(h, 1), :], coarse[s, 1, pl.ds(h, 1), :]
        at = pl.ds(pl.multiple_of(h * 64, 64), 64)
        ref[at, 0:K] = (are * bre - aim * bim).astype(BF)
        ref[at, K : 2 * K] = (are * bim + aim * bre).astype(BF)

    def image_of(s, f):
        cos, sin = cis(off_ref[0, s] * (FACET * (2 * fx + f) + iota((1, FR), 1)))
        qre, qim = qre_v[...], qim_v[...]
        ure, uim = qre * cos + qim * sin, qim * cos - qre * sin
        if f == 1:
            sign = jnp.where((iota((K, 1), 0) & 1) == 1, -1.0, 1.0)
            ure, uim = ure * sign, uim * sign
        table = jnp.concatenate([ure, uim], 0).astype(BF)
        strips = acc[f].astype(BF)
        mixed = jnp.dot(table, strips, preferred_element_type=F32)
        bre = mixed[:K, :K] - mixed[K:, K:]
        bim = mixed[:K, K:] + mixed[K:, :K]
        block = jnp.concatenate([bre, bim], 1).astype(BF)
        image = jnp.dot(block, dc[...], preferred_element_type=F32)
        images[f, :, 0:K] = image[:, :K].T.astype(BF)
        images[f, :, K : 2 * K] = image[:, K:].T.astype(BF)

    def window_of(s):
        both = jnp.concatenate([images[0], images[1]], 1)
        window = jnp.dot(both, dr[...], preferred_element_type=F32).astype(BF)
        for k in range(12):
            di, dj = divmod(k, 4)
            at = halo_ks.index(k) if k in halo_ks else 11
            pieces[s, at] = window[32 * dj : 32 * dj + 32, 128 * di : 128 * di + 128]

    def finish(s, f):
        image_of(s, f)
        if f == 1:
            window_of(s)
            if s == 0:
                pl.semaphore_wait(barrier, 33)
            for k in range(11):
                halo_copy(s, k).start()
            if s >= 2:
                sum_halo(s - 2)

    def sum_halo(s):
        wait_for(halo_sems.at[s], halo.at[s])
        total = pieces[s, 11].astype(F32)
        for k in range(11):
            total = total + halo[s, k].astype(F32)
        plane[s, own] = total.astype(BF)
        for k in range(15):
            plane_copy(s, k).start()

    @pl.loop(0, 16)
    def _(h):
        for d in range(4):
            fill(0, 4 * h + d, va)

    for load in loads[:4]:
        load.wait()
    for s in range(NSUB):
        table, after = (va, vb) if s % 2 == 0 else (vb, va)
        for f in range(2):
            if s == 0:
                for c in range(CHUNKS // 2):
                    sky_copy(f * CHUNKS // 2 + c).wait()
            rows_of_facet = sky_v[FR * f : FR * f + FR, :]
            acc[f] = jnp.dot(rows_of_facet, table[...], preferred_element_type=F32)
            if s + 1 < NSUB:
                for h in range(32):
                    fill(s + 1, 32 * f + h, after)
            if f == 1:
                finish(s, 0)
            elif s > 0:
                finish(s - 1, 1)
    finish(NSUB - 1, 1)

    for load in loads[4:]:
        load.wait()
    tiles = cells.shape[1] // VTILE

    @pl.loop(0, tiles)
    def _(t):
        at = pl.ds(pl.multiple_of(t * VTILE, VTILE), VTILE)
        laid, block = turned(rows[:, at].astype(F32), cells[0:1, at])
        across = iota((SUB // 8, 8, VTILE), 0)
        weights = jnp.where(across == block[None], laid[None], 0.0)
        spread[:, at] = weights.reshape(SUB, VTILE).astype(BF)
        laid, block = turned(cols[:, at], cells[1:2, at])
        taps[:, at] = laid
        blocks[:, at] = block

    sum_halo(2)
    sum_halo(3)
    for s in range(NSUB):
        wait_for(plane_sems.at[s], plane.at[s, 0:15])
    for k in range(7):
        peer = last_to[k]
        outbox[k] = plane[readers_ref[peer[0] * 16 + peer[1]]]
        last_copy(k, mine).start()
    fin[mine] = plane[readers_ref[fx * 16 + fy]]
    for k in range(7):
        last_copy(k, last_peer(k + 1, -1)[1]).wait_recv()

    for i in range(8):
        for j in range(16):
            a, b = place_of(i, j)
            lhs[32 * j : 32 * j + 32, 128 * i : 128 * i + 128] = fin[a, b]
    for h in range(2):
        at = slice(SUB * h, SUB * h + SUB)
        yy[at] = jnp.dot(lhs[...], et[:, at], preferred_element_type=F32).astype(BF)
    for h in range(2):
        at = slice(SUB * h, SUB * h + SUB)
        grid_t[at] = jnp.dot(en[at], yy[...], preferred_element_type=F32).astype(BF)

    @pl.loop(0, tiles)
    def _(t):
        at = pl.ds(pl.multiple_of(t * VTILE, VTILE), VTILE)
        block = blocks[:, at]
        sums = [jnp.zeros((8, VTILE), F32), jnp.zeros((8, VTILE), F32)]
        for c in range(4):
            here = (iota((16, 8, VTILE), 0) + 16 * c) == block[None]
            for p in range(2):
                part = grid_t[SUB * p + 128 * c : SUB * p + 128 * c + 128]
                values = jnp.dot(part, spread[:, at], preferred_element_type=F32)
                values = values.reshape(16, 8, VTILE)
                sums[p] = sums[p] + jnp.sum(jnp.where(here, values, 0.0), axis=0)
        for p in range(2):
            out_ref[p : p + 1, at] = jnp.sum(sums[p] * taps[:, at], axis=0, keepdims=True)

    wait_for(send_sems.at[0], halo)
    wait_for(send_sems.at[1], plane.at[:, 0:15])
    wait_for(send_sems.at[2], outbox)


def local(sky, sub_off, readers, vis_cells, row_kernel, col_kernel):
    hbm = pl.BlockSpec(memory_space=pltpu.HBM)
    smem = pl.BlockSpec(memory_space=pltpu.SMEM)
    count = vis_cells.shape[1]
    return pl.pallas_call(
        kernel,
        out_shape=jax.ShapeDtypeStruct((2, count), F32),
        in_specs=[hbm, smem, smem] + [hbm] * 9,
        out_specs=pl.BlockSpec(memory_space=pltpu.VMEM),
        scratch_shapes=[
            pltpu.VMEM((2 * FR, FACET), BF),
            pltpu.VMEM((FACET, 2 * K), BF),
            pltpu.VMEM((FACET, 2 * K), BF),
            pltpu.VMEM((2, FR, 2 * K), F32),
            pltpu.VMEM((NSUB, 2, 64, K), F32),
            pltpu.VMEM((NSUB, 2, 64, K), F32),
            pltpu.VMEM((2, K, 2 * K), BF),
            pltpu.VMEM((NSUB, 12, 32, 128), BF),
            pltpu.VMEM((NSUB, 11, 32, 128), BF),
            pltpu.VMEM((NSUB, 16, 32, 128), BF),
            pltpu.VMEM((7, 16, 32, 128), BF),
            pltpu.VMEM((8, 16, 32, 128), BF),
            pltpu.VMEM((SUB, 2 * SUB), BF),
            pltpu.VMEM((2 * SUB, SUB), BF),
            pltpu.VMEM((2 * SUB, SUB), BF),
            pltpu.VMEM((SUB, count), BF),
            pltpu.VMEM((8, count), F32),
            pltpu.VMEM((8, count), jnp.int32),
            pltpu.VMEM((2 * SUB, 2 * SUB), BF),
            pltpu.VMEM((2 * SUB, 2 * SUB), BF),
            pltpu.VMEM((2 * K, 2 * K), BF),
            pltpu.VMEM((4 * K, 384), BF),
            pltpu.VMEM((K, FR), F32),
            pltpu.VMEM((K, FR), F32),
            pltpu.VMEM((2, count), jnp.int32),
            pltpu.VMEM((8, count), BF),
            pltpu.VMEM((8, count), F32),
            pltpu.SemaphoreType.DMA((CHUNKS,)),
            pltpu.SemaphoreType.DMA((9,)),
            pltpu.SemaphoreType.DMA((3,)),
            pltpu.SemaphoreType.DMA((NSUB,)),
            pltpu.SemaphoreType.DMA((NSUB,)),
            pltpu.SemaphoreType.DMA((7,)),
        ],
        compiler_params=pltpu.CompilerParams(
            collective_id=0, has_side_effects=True, vmem_limit_bytes=56 * 2**20
        ),
    )(sky, sub_off, readers, vis_cells, row_kernel, col_kernel, *small_tables(), *grid_tables())


def solution(mesh):
    return jax.shard_map(
        local,
        mesh=mesh,
        in_specs=(
            P("fx", "fy"),
            P(),
            P(),
            P(None, ("fx", "fy")),
            P(None, ("fx", "fy")),
            P(None, ("fx", "fy")),
        ),
        out_specs=P(None, ("fx", "fy")),
        check_vma=False,
    )
```

```python
import math

import jax
import jax.numpy as jnp
import numpy as np
from jax import lax
from jax.experimental import pallas as pl
from jax.experimental.pallas import tpu as pltpu
from jax.sharding import PartitionSpec as P

FACET = 4096
SUB = 512
K = 128
W = 8
FR = 512
NSUB = 4
SKY = 65536
CHUNK = 256
CHUNKS = 2 * FR // CHUNK
VTILE = 256
BF = jnp.bfloat16
F32 = jnp.float32
MESH = pl.DeviceIdType.MESH


def wave(rows, cols, period):
    turn = (np.arange(rows)[:, None] * np.arange(cols)[None, :]) % period
    angle = turn * (2.0 * math.pi / period)
    return np.cos(angle), np.sin(angle)


def small_tables():
    re, im = wave(K, K, K)
    re, im = re / K, -im / K
    cols = np.block([[re.T, im.T], [-im.T, re.T]])
    rows = np.zeros((2, 2, K, 3, 2, 64))
    for f in range(2):
        for t in range(K):
            at, cell = divmod(32 * f + t, 64)
            rows[f, 0, :, at, 0, cell] = re[t]
            rows[f, 1, :, at, 0, cell] = -im[t]
            rows[f, 0, :, at, 1, cell] = im[t]
            rows[f, 1, :, at, 1, cell] = re[t]
    qre, qim = wave(K, FR, SKY // 4)
    scale = 1.0 / math.sqrt(FR)
    return (
        jnp.asarray(cols, BF),
        jnp.asarray(rows.reshape(4 * K, 384), BF),
        jnp.asarray(qre * scale, F32),
        jnp.asarray(-qim * scale, F32),
    )


def grid_tables():
    half = SUB // 2
    re, im = wave(SUB, half, SUB)
    et, en = [], []
    for r in range(2):
        a, b = re[r::2], im[r::2]
        rows = np.stack([np.concatenate([a.T, b.T], 1), np.concatenate([-b.T, a.T], 1)])
        et.append(rows.reshape(2, 4, 64, SUB).transpose(1, 0, 2, 3).reshape(SUB, SUB))
        en.append(np.block([[a, -b], [b, a]]) / 16.0)
    return jnp.asarray(np.stack(et), BF), jnp.asarray(np.stack(en), BF)


def cis(phase):
    turn = phase & 0xFFFF
    quarter = (turn + 8192) >> 14
    x = (turn - (quarter << 14)).astype(F32) * (2.0 * math.pi / SKY)
    x2 = x * x
    c = 1.0 + x2 * (-0.5 + x2 * (1.0 / 24 + x2 * (-1.0 / 720 + x2 * (1.0 / 40320))))
    s = x * (1.0 + x2 * (-1.0 / 6 + x2 * (1.0 / 120 + x2 * (-1.0 / 5040 + x2 * (1.0 / 362880)))))
    odd = (quarter & 1) == 1
    cos = jnp.where(odd, s, c)
    sin = jnp.where(odd, c, s)
    cos = jnp.where(((quarter + 1) & 2) != 0, -cos, cos)
    sin = jnp.where((quarter & 2) != 0, -sin, sin)
    return cos, sin


def iota(shape, dim):
    return lax.broadcasted_iota(jnp.int32, shape, dim)


def turned(kernel, start, r):
    head = (start + 1 - r) >> 1
    first = head & 7
    even = jnp.concatenate([kernel[e : e + 1] for e in (0, 2, 4, 6)], 0)
    odd = jnp.concatenate([kernel[e : e + 1] for e in (1, 3, 5, 7)], 0)
    taps = jnp.where(((start + r) & 1) == 0, even, odd)
    taps = jnp.concatenate([taps, jnp.zeros_like(taps)], 0)
    laid = taps
    for turn in range(1, 8):
        laid = jnp.where(first == turn, jnp.roll(taps, turn, 0), laid)
    return laid, (head >> 3) + jnp.where(iota(taps.shape, 0) < first, 1, 0)


def place_of(i, j):
    j = (j + 15) % 16
    x, y, z, core = 2 * (j // 8) + i % 2, i // 2, (j // 2) % 4, j % 2
    return (4 + z, x * 4 + y) if core else (x, z * 4 + y)


def kernel(
    sky_ref, off_ref, readers_ref, cells_ref, rows_ref, cols_ref,
    dc_ref, dr_ref, qre_ref, qim_ref, et_ref, en_ref, out_ref,
    sky_v, va, vb, acc, coarse, fine, mid, images, pieces, halo, plane, outbox, fin,
    lhs, yy, grid_t, spread, taps, blocks, et, en, dc, dr, qre_v, qim_v, cells, rows, cols,
    sky_sems, load_sems, send_sems, halo_sems, plane_sems, last_sems,
):
    fx, fy = lax.axis_index("fx"), lax.axis_index("fy")
    y, core, z = fx // 2, fy % 2, (fy // 2) % 4
    x = 2 * (fy // 8) + fx % 2
    first = core == 0

    def sky_copy(c):
        part = pl.ds(c * CHUNK, CHUNK)
        return pltpu.make_async_copy(sky_ref.at[part], sky_v.at[part], sky_sems.at[c])

    moves = [
        (dc_ref, dc), (dr_ref, dr), (qre_ref, qre_v), (qim_ref, qim_v),
        (cells_ref, cells), (rows_ref, rows), (cols_ref, cols), (et_ref, et), (en_ref, en),
    ]
    loads = [
        pltpu.make_async_copy(src, dst, load_sems.at[n]) for n, (src, dst) in enumerate(moves)
    ]
    for c in range(CHUNKS):
        sky_copy(c).start()
    for load in loads:
        load.start()

    def device(x, y, z, core):
        return (2 * y + x % 2, (x // 2) * 8 + 2 * z + core)

    def axis_of(core):
        return jnp.where(core == 0, x, z)

    def halo_peer(k, sign):
        return ((fx + sign * (k // 4) + 8) % 8, (fy + sign * (k % 4 - 1) + 16) % 16)

    def plane_peer(k, sign):
        far = (jnp.where(first, z, x) + sign * (k // 4) + 4) % 4
        yy = (y + sign * (k % 4) + 4) % 4
        return device(jnp.where(first, x, far), yy, jnp.where(first, far, z), core), far * 4 + yy

    def last_peer(k, sign):
        other = (core + k % 2) % 2
        mover = core if sign == 1 else other
        place = (axis_of(mover) + sign * (k // 2) + 4) % 4
        xx, zz = jnp.where(mover == 0, place, x), jnp.where(mover == 0, z, place)
        slot = mover * 4 + (axis_of(mover) if sign == 1 else place)
        return device(xx, y, zz, other), slot

    halo_ks = [k for k in range(12) if k != 1]
    halo_to = [halo_peer(k, 1) for k in halo_ks]
    plane_to = [plane_peer(k, 1)[0] for k in range(1, 16)]
    last_to = [last_peer(k, 1)[0] for k in range(1, 8)]
    barrier = pltpu.get_barrier_semaphore()
    for k in halo_ks:
        pl.semaphore_signal(barrier, inc=1, device_id=halo_peer(k, -1), device_id_type=MESH)
    for k in range(1, 16):
        pl.semaphore_signal(barrier, inc=1, device_id=plane_peer(k, -1)[0], device_id_type=MESH)
    for k in range(1, 8):
        pl.semaphore_signal(barrier, inc=1, device_id=last_peer(k, -1)[0], device_id_type=MESH)

    own = jnp.where(first, z, x) * 4 + y
    mine = core * 4 + axis_of(core)

    def halo_copy(s, k):
        return pltpu.make_async_remote_copy(
            src_ref=pieces.at[s, k], dst_ref=halo.at[s, k],
            send_sem=send_sems.at[0], recv_sem=halo_sems.at[s],
            device_id=halo_to[k], device_id_type=MESH,
        )

    def plane_copy(s, k):
        return pltpu.make_async_remote_copy(
            src_ref=plane.at[s, own], dst_ref=plane.at[s, own],
            send_sem=send_sems.at[1], recv_sem=plane_sems.at[s],
            device_id=plane_to[k], device_id_type=MESH,
        )

    def last_copy(k, slot):
        return pltpu.make_async_remote_copy(
            src_ref=outbox.at[k], dst_ref=fin.at[slot],
            send_sem=send_sems.at[2], recv_sem=last_sems.at[k],
            device_id=last_to[k], device_id_type=MESH,
        )

    def wait_for(sem, ref):
        pltpu.make_async_copy(ref, ref, sem).wait()

    step, lane = iota((64, K), 0), iota((64, K), 1)
    for s in range(NSUB):
        freq = off_ref[1, s] + 4 * lane
        cos, sin = cis(freq * (64 * step + FACET * fy) + SKY // 4 * lane * fy)
        coarse[s, 0] = cos
        coarse[s, 1] = -sin
        cos, sin = cis(freq * step)
        fine[s, 0] = cos * (1.0 / 64)
        fine[s, 1] = -sin * (1.0 / 64)

    def fill(s, h, ref):
        bre, bim = fine[s, 0], fine[s, 1]
        are, aim = coarse[s, 0, pl.ds(h, 1), :], coarse[s, 1, pl.ds(h, 1), :]
        at = pl.ds(pl.multiple_of(h * 64, 64), 64)
        ref[at, 0:K] = (are * bre - aim * bim).astype(BF)
        ref[at, K : 2 * K] = (are * bim + aim * bre).astype(BF)

    def mix(s, f):
        cos, sin = cis(off_ref[0, s] * (FACET * (2 * fx + f) + iota((1, FR), 1)))
        qre, qim = qre_v[...], qim_v[...]
        ure, uim = qre * cos + qim * sin, qim * cos - qre * sin
        if f == 1:
            sign = jnp.where((iota((K, 1), 0) & 1) == 1, -1.0, 1.0)
            ure, uim = ure * sign, uim * sign
        table = jnp.concatenate([ure, uim], 0).astype(BF)
        mixed = jnp.dot(table, acc[f].astype(BF), preferred_element_type=F32)
        mid[f, :, 0:K] = (mixed[:K, :K] - mixed[K:, K:]).astype(BF)
        mid[f, :, K : 2 * K] = (mixed[:K, K:] + mixed[K:, :K]).astype(BF)

    def image_of(f):
        image = jnp.dot(mid[f], dc[...], preferred_element_type=F32)
        images[:, 2 * K * f : 2 * K * f + K] = image[:, :K].T.astype(BF)
        images[:, 2 * K * f + K : 2 * K * f + 2 * K] = image[:, K:].T.astype(BF)

    def window_of(s):
        window = jnp.dot(images[...], dr[...], preferred_element_type=F32).astype(BF)
        for k in range(12):
            di, dj = divmod(k, 4)
            at = halo_ks.index(k) if k in halo_ks else 11
            pieces[s, at] = window[32 * dj : 32 * dj + 32, 128 * di : 128 * di + 128]
        if s == 0:
            pl.semaphore_wait(barrier, 33)
        for k in range(11):
            halo_copy(s, k).start()

    def sum_halo(s):
        wait_for(halo_sems.at[s], halo.at[s])
        total = pieces[s, 11].astype(F32)
        for k in range(11):
            total = total + halo[s, k].astype(F32)
        plane[s, own] = total.astype(BF)
        for k in range(15):
            plane_copy(s, k).start()

    @pl.loop(0, 16)
    def _(h):
        for d in range(4):
            fill(0, 4 * h + d, va)

    for load in loads[:4]:
        load.wait()
    for s in range(NSUB):
        table, after = (va, vb) if s % 2 == 0 else (vb, va)
        for f in range(2):
            if s == 0:
                for c in range(CHUNKS // 2):
                    sky_copy(f * CHUNKS // 2 + c).wait()
            rows_of_facet = sky_v[FR * f : FR * f + FR, :]
            acc[f] = jnp.dot(rows_of_facet, table[...], preferred_element_type=F32)
            if s + 1 < NSUB:
                for h in range(32):
                    fill(s + 1, 32 * f + h, after)
            turn = 2 * s + f
            if turn >= 4 and f == 0:
                window_of(s - 2)
            if turn >= 1:
                mix((turn - 1) // 2, (turn - 1) % 2)
            if turn >= 2:
                image_of(turn % 2)
    mix(NSUB - 1, 1)
    window_of(NSUB - 2)
    image_of(0)
    image_of(1)
    window_of(NSUB - 1)
    sum_halo(0)
    sum_halo(1)

    for load in loads[4:]:
        load.wait()
    tiles = cells.shape[1] // VTILE

    @pl.loop(0, tiles)
    def _(t):
        at = pl.ds(pl.multiple_of(t * VTILE, VTILE), VTILE)
        for r in range(2):
            laid, block = turned(rows[:, at].astype(F32), cells[0:1, at], r)
            across = iota((SUB // 16, 8, VTILE), 0)
            weights = jnp.where(across == block[None], laid[None], 0.0)
            spread[256 * r : 256 * r + 256, at] = weights.reshape(SUB // 2, VTILE).astype(BF)
            laid, block = turned(cols[:, at], cells[1:2, at], r)
            taps[r, :, at] = laid
            blocks[r, :, at] = block

    sum_halo(2)
    sum_halo(3)
    for s in range(NSUB):
        wait_for(plane_sems.at[s], plane.at[s, 0:15])
    for k in range(7):
        peer = last_to[k]
        outbox[k] = plane[readers_ref[peer[0] * 16 + peer[1]]]
        last_copy(k, mine).start()
    fin[mine] = plane[readers_ref[fx * 16 + fy]]
    for k in range(7):
        last_copy(k, last_peer(k + 1, -1)[1]).wait_recv()

    for i in range(4):
        for j in range(16):
            low, high = (fin[place_of(h, j)].astype(F32) for h in (i, i + 4))
            at = (slice(32 * j, 32 * j + 32), slice(128 * i, 128 * i + 128))
            lhs[0, at[0], at[1]] = (low + high).astype(BF)
            lhs[1, at[0], at[1]] = (low - high).astype(BF)
    for r in range(2):
        for p in range(2):
            part = et[r, :, 256 * p : 256 * p + 256]
            done = jnp.dot(lhs[r], part, preferred_element_type=F32)
            low, high = done[:256], done[256:]
            at = (slice(256 * p, 256 * p + 256), slice(256 * r, 256 * r + 256))
            yy[0, at[0], at[1]] = (low + high).astype(BF)
            yy[1, at[0], at[1]] = (low - high).astype(BF)
    for r in range(2):
        grid_t[r] = jnp.dot(en[r], yy[r], preferred_element_type=F32).astype(BF)

    @pl.loop(0, tiles)
    def _(t):
        at = pl.ds(pl.multiple_of(t * VTILE, VTILE), VTILE)
        totals = [0.0, 0.0]
        for r in range(2):
            block = blocks[r, :, at]
            sums = [jnp.zeros((8, VTILE), F32), jnp.zeros((8, VTILE), F32)]
            for c in range(2):
                here = (iota((16, 8, VTILE), 0) + 16 * c) == block[None]
                for p in range(2):
                    part = grid_t[r, 256 * p + 128 * c : 256 * p + 128 * c + 128]
                    values = jnp.dot(part, spread[:, at], preferred_element_type=F32)
                    values = values.reshape(16, 8, VTILE)
                    sums[p] = sums[p] + jnp.sum(jnp.where(here, values, 0.0), axis=0)
            for p in range(2):
                totals[p] = totals[p] + sums[p] * taps[r, :, at]
        for p in range(2):
            out_ref[p : p + 1, at] = jnp.sum(totals[p], axis=0, keepdims=True)

    wait_for(send_sems.at[0], halo)
    wait_for(send_sems.at[1], plane.at[:, 0:15])
    wait_for(send_sems.at[2], outbox)


def local(sky, sub_off, readers, vis_cells, row_kernel, col_kernel):
    hbm = pl.BlockSpec(memory_space=pltpu.HBM)
    smem = pl.BlockSpec(memory_space=pltpu.SMEM)
    count = vis_cells.shape[1]
    return pl.pallas_call(
        kernel,
        out_shape=jax.ShapeDtypeStruct((2, count), F32),
        in_specs=[hbm, smem, smem] + [hbm] * 9,
        out_specs=pl.BlockSpec(memory_space=pltpu.VMEM),
        scratch_shapes=[
            pltpu.VMEM((2 * FR, FACET), BF),
            pltpu.VMEM((FACET, 2 * K), BF),
            pltpu.VMEM((FACET, 2 * K), BF),
            pltpu.VMEM((2, FR, 2 * K), F32),
            pltpu.VMEM((NSUB, 2, 64, K), F32),
            pltpu.VMEM((NSUB, 2, 64, K), F32),
            pltpu.VMEM((2, K, 2 * K), BF),
            pltpu.VMEM((K, 4 * K), BF),
            pltpu.VMEM((NSUB, 12, 32, 128), BF),
            pltpu.VMEM((NSUB, 11, 32, 128), BF),
            pltpu.VMEM((NSUB, 16, 32, 128), BF),
            pltpu.VMEM((7, 16, 32, 128), BF),
            pltpu.VMEM((8, 16, 32, 128), BF),
            pltpu.VMEM((2, SUB, SUB), BF),
            pltpu.VMEM((2, SUB, SUB), BF),
            pltpu.VMEM((2, SUB, SUB), BF),
            pltpu.VMEM((SUB, count), BF),
            pltpu.VMEM((2, 8, count), F32),
            pltpu.VMEM((2, 8, count), jnp.int32),
            pltpu.VMEM((2, SUB, SUB), BF),
            pltpu.VMEM((2, SUB, SUB), BF),
            pltpu.VMEM((2 * K, 2 * K), BF),
            pltpu.VMEM((4 * K, 384), BF),
            pltpu.VMEM((K, FR), F32),
            pltpu.VMEM((K, FR), F32),
            pltpu.VMEM((2, count), jnp.int32),
            pltpu.VMEM((8, count), BF),
            pltpu.VMEM((8, count), F32),
            pltpu.SemaphoreType.DMA((CHUNKS,)),
            pltpu.SemaphoreType.DMA((9,)),
            pltpu.SemaphoreType.DMA((3,)),
            pltpu.SemaphoreType.DMA((NSUB,)),
            pltpu.SemaphoreType.DMA((NSUB,)),
            pltpu.SemaphoreType.DMA((7,)),
        ],
        compiler_params=pltpu.CompilerParams(
            collective_id=0, has_side_effects=True, vmem_limit_bytes=56 * 2**20
        ),
    )(sky, sub_off, readers, vis_cells, row_kernel, col_kernel, *small_tables(), *grid_tables())


def solution(mesh):
    return jax.shard_map(
        local,
        mesh=mesh,
        in_specs=(
            P("fx", "fy"),
            P(),
            P(),
            P(None, ("fx", "fy")),
            P(None, ("fx", "fy")),
            P(None, ("fx", "fy")),
        ),
        out_specs=P(None, ("fx", "fy")),
        check_vma=False,
    )
```

```python
import math

import jax
import jax.numpy as jnp
import numpy as np
from jax import lax
from jax.experimental import pallas as pl
from jax.experimental.pallas import tpu as pltpu
from jax.sharding import PartitionSpec as P

FACET = 4096
SUB = 512
K = 128
W = 8
FR = 512
NSUB = 4
SKY = 65536
CHUNK = 256
CHUNKS = 2 * FR // CHUNK
VTILE = 256
BF = jnp.bfloat16
F32 = jnp.float32
MESH = pl.DeviceIdType.MESH


def wave(rows, cols, period):
    turn = (np.arange(rows)[:, None] * np.arange(cols)[None, :]) % period
    angle = turn * (2.0 * math.pi / period)
    return np.cos(angle), np.sin(angle)


def small_tables():
    re, im = wave(K, K, K)
    re, im = re / K, -im / K
    cols = np.block([[re.T, im.T], [-im.T, re.T]])
    rows = np.zeros((2, 2, K, 3, 2, 64))
    for f in range(2):
        for t in range(K):
            at, cell = divmod(32 * f + t, 64)
            rows[f, 0, :, at, 0, cell] = re[t]
            rows[f, 1, :, at, 0, cell] = -im[t]
            rows[f, 0, :, at, 1, cell] = im[t]
            rows[f, 1, :, at, 1, cell] = re[t]
    qre, qim = wave(K, FR, SKY // 4)
    scale = 1.0 / math.sqrt(FR)
    return (
        jnp.asarray(cols, BF),
        jnp.asarray(rows.reshape(4 * K, 384), BF),
        jnp.asarray(qre * scale, F32),
        jnp.asarray(-qim * scale, F32),
    )


def grid_tables():
    half = SUB // 2
    re, im = wave(SUB, half, SUB)
    et, en = [], []
    for r in range(2):
        a, b = re[r::2], im[r::2]
        rows = np.stack([np.concatenate([a.T, b.T], 1), np.concatenate([-b.T, a.T], 1)])
        et.append(rows.reshape(2, 4, 64, SUB).transpose(1, 0, 2, 3).reshape(SUB, SUB))
        en.append(np.block([[a, -b], [b, a]]) / 16.0)
    return jnp.asarray(np.stack(et), BF), jnp.asarray(np.stack(en), BF)


def cis(phase):
    turn = phase & 0xFFFF
    quarter = (turn + 8192) >> 14
    x = (turn - (quarter << 14)).astype(F32) * (2.0 * math.pi / SKY)
    x2 = x * x
    c = 1.0 + x2 * (-0.5 + x2 * (1.0 / 24 + x2 * (-1.0 / 720 + x2 * (1.0 / 40320))))
    s = x * (1.0 + x2 * (-1.0 / 6 + x2 * (1.0 / 120 + x2 * (-1.0 / 5040 + x2 * (1.0 / 362880)))))
    odd = (quarter & 1) == 1
    cos = jnp.where(odd, s, c)
    sin = jnp.where(odd, c, s)
    cos = jnp.where(((quarter + 1) & 2) != 0, -cos, cos)
    sin = jnp.where((quarter & 2) != 0, -sin, sin)
    return cos, sin


def iota(shape, dim):
    return lax.broadcasted_iota(jnp.int32, shape, dim)


def turned(kernel, start, r):
    head = (start + 1 - r) >> 1
    first = head & 7
    even = jnp.concatenate([kernel[e : e + 1] for e in (0, 2, 4, 6)], 0)
    odd = jnp.concatenate([kernel[e : e + 1] for e in (1, 3, 5, 7)], 0)
    taps = jnp.where(((start + r) & 1) == 0, even, odd)
    taps = jnp.concatenate([taps, jnp.zeros_like(taps)], 0)
    laid = taps
    for turn in range(1, 8):
        laid = jnp.where(first == turn, jnp.roll(taps, turn, 0), laid)
    return laid, (head >> 3) + jnp.where(iota(taps.shape, 0) < first, 1, 0)


def place_of(i, j):
    j = (j + 15) % 16
    x, y, z, core = 2 * (j // 8) + i % 2, i // 2, (j // 2) % 4, j % 2
    return (4 + z, x * 4 + y) if core else (x, z * 4 + y)


def kernel(
    sky_ref, off_ref, readers_ref, cells_ref, rows_ref, cols_ref,
    dc_ref, dr_ref, qre_ref, qim_ref, et_ref, en_ref, out_ref,
    sky_v, va, vb, acc, coarse, fine, mid, images, pieces, halo, plane, outbox, fin,
    lhs, yy, grid_t, spread, taps, blocks, et, en, dc, dr, qre_v, qim_v, cells, rows, cols,
    sky_sems, load_sems, send_sems, halo_sems, plane_sems, last_sems,
):
    fx, fy = lax.axis_index("fx"), lax.axis_index("fy")
    y, core, z = fx // 2, fy % 2, (fy // 2) % 4
    x = 2 * (fy // 8) + fx % 2
    first = core == 0

    def sky_copy(c):
        part = pl.ds(c * CHUNK, CHUNK)
        return pltpu.make_async_copy(sky_ref.at[part], sky_v.at[part], sky_sems.at[c])

    moves = [
        (dc_ref, dc), (dr_ref, dr), (qre_ref, qre_v), (qim_ref, qim_v),
        (cells_ref, cells), (rows_ref, rows), (cols_ref, cols), (et_ref, et), (en_ref, en),
    ]
    loads = [
        pltpu.make_async_copy(src, dst, load_sems.at[n]) for n, (src, dst) in enumerate(moves)
    ]
    for c in range(CHUNKS):
        sky_copy(c).start()
        if c == CHUNKS // 2 - 1:
            for load in loads[:4]:
                load.start()
    for load in loads[4:]:
        load.start()

    def device(x, y, z, core):
        return (2 * y + x % 2, (x // 2) * 8 + 2 * z + core)

    def axis_of(core):
        return jnp.where(core == 0, x, z)

    def halo_peer(k, sign):
        return ((fx + sign * (k // 4) + 8) % 8, (fy + sign * (k % 4 - 1) + 16) % 16)

    def plane_peer(k, sign):
        far = (jnp.where(first, z, x) + sign * (k // 4) + 4) % 4
        yy = (y + sign * (k % 4) + 4) % 4
        return device(jnp.where(first, x, far), yy, jnp.where(first, far, z), core), far * 4 + yy

    def last_peer(k, sign):
        other = (core + k % 2) % 2
        mover = core if sign == 1 else other
        place = (axis_of(mover) + sign * (k // 2) + 4) % 4
        xx, zz = jnp.where(mover == 0, place, x), jnp.where(mover == 0, z, place)
        slot = mover * 4 + (axis_of(mover) if sign == 1 else place)
        return device(xx, y, zz, other), slot

    halo_ks = [k for k in range(12) if k != 1]
    halo_to = [halo_peer(k, 1) for k in halo_ks]
    plane_to = [plane_peer(k, 1)[0] for k in range(1, 16)]
    last_to = [last_peer(k, 1)[0] for k in range(1, 8)]
    barrier = pltpu.get_barrier_semaphore()
    for k in halo_ks:
        pl.semaphore_signal(barrier, inc=1, device_id=halo_peer(k, -1), device_id_type=MESH)
    for k in range(1, 16):
        pl.semaphore_signal(barrier, inc=1, device_id=plane_peer(k, -1)[0], device_id_type=MESH)
    for k in range(1, 8):
        pl.semaphore_signal(barrier, inc=1, device_id=last_peer(k, -1)[0], device_id_type=MESH)

    own = jnp.where(first, z, x) * 4 + y
    mine = core * 4 + axis_of(core)

    def halo_copy(s, k):
        return pltpu.make_async_remote_copy(
            src_ref=pieces.at[s, k], dst_ref=halo.at[s, k],
            send_sem=send_sems.at[0], recv_sem=halo_sems.at[s],
            device_id=halo_to[k], device_id_type=MESH,
        )

    def plane_copy(s, k):
        return pltpu.make_async_remote_copy(
            src_ref=plane.at[s, own], dst_ref=plane.at[s, own],
            send_sem=send_sems.at[1], recv_sem=plane_sems.at[s],
            device_id=plane_to[k], device_id_type=MESH,
        )

    def last_copy(k, slot):
        return pltpu.make_async_remote_copy(
            src_ref=outbox.at[k], dst_ref=fin.at[slot],
            send_sem=send_sems.at[2], recv_sem=last_sems.at[k],
            device_id=last_to[k], device_id_type=MESH,
        )

    def wait_for(sem, ref):
        pltpu.make_async_copy(ref, ref, sem).wait()

    step, lane = iota((64, K), 0), iota((64, K), 1)
    for s in range(NSUB):
        freq = off_ref[1, s] + 4 * lane
        cos, sin = cis(freq * (64 * step + FACET * fy) + SKY // 4 * lane * fy)
        coarse[s, 0] = cos
        coarse[s, 1] = -sin
        cos, sin = cis(freq * step)
        fine[s, 0] = cos * (1.0 / 64)
        fine[s, 1] = -sin * (1.0 / 64)

    def fill(s, h, ref):
        bre, bim = fine[s, 0], fine[s, 1]
        are, aim = coarse[s, 0, pl.ds(h, 1), :], coarse[s, 1, pl.ds(h, 1), :]
        at = pl.ds(pl.multiple_of(h * 64, 64), 64)
        ref[at, 0:K] = (are * bre - aim * bim).astype(BF)
        ref[at, K : 2 * K] = (are * bim + aim * bre).astype(BF)

    def mix(s, f):
        cos, sin = cis(off_ref[0, s] * (FACET * (2 * fx + f) + iota((1, FR), 1)))
        qre, qim = qre_v[...], qim_v[...]
        ure, uim = qre * cos + qim * sin, qim * cos - qre * sin
        if f == 1:
            sign = jnp.where((iota((K, 1), 0) & 1) == 1, -1.0, 1.0)
            ure, uim = ure * sign, uim * sign
        table = jnp.concatenate([ure, uim], 0).astype(BF)
        mixed = jnp.dot(table, acc[f].astype(BF), preferred_element_type=F32)
        mid[f, :, 0:K] = (mixed[:K, :K] - mixed[K:, K:]).astype(BF)
        mid[f, :, K : 2 * K] = (mixed[:K, K:] + mixed[K:, :K]).astype(BF)

    def image_of(f):
        image = jnp.dot(mid[f], dc[...], preferred_element_type=F32)
        images[:, 2 * K * f : 2 * K * f + K] = image[:, :K].T.astype(BF)
        images[:, 2 * K * f + K : 2 * K * f + 2 * K] = image[:, K:].T.astype(BF)

    def window_of(s):
        window = jnp.dot(images[...], dr[...], preferred_element_type=F32).astype(BF)
        for k in range(12):
            di, dj = divmod(k, 4)
            at = halo_ks.index(k) if k in halo_ks else 11
            pieces[s, at] = window[32 * dj : 32 * dj + 32, 128 * di : 128 * di + 128]

    def send_halo(s):
        for k in range(11):
            halo_copy(s, k).start()

    def sum_halo(s):
        wait_for(halo_sems.at[s], halo.at[s])
        total = pieces[s, 11].astype(F32)
        for k in range(11):
            total = total + halo[s, k].astype(F32)
        plane[s, own] = total.astype(BF)
        for k in range(15):
            plane_copy(s, k).start()

    @pl.loop(0, 16)
    def _(h):
        for d in range(4):
            fill(0, 4 * h + d, va)

    for s in range(NSUB):
        table, after = (va, vb) if s % 2 == 0 else (vb, va)
        for f in range(2):
            if s == 0:
                for c in range(CHUNKS // 2):
                    sky_copy(f * CHUNKS // 2 + c).wait()
            if 2 * s + f == 7:
                pl.semaphore_wait(barrier, 33)
                for t in range(2):
                    send_halo(t)
            rows_of_facet = sky_v[FR * f : FR * f + FR, :]
            acc[f] = jnp.dot(rows_of_facet, table[...], preferred_element_type=F32)
            if s + 1 < NSUB:
                for h in range(32):
                    fill(s + 1, 32 * f + h, after)
            turn = 2 * s + f
            if turn >= 4 and f == 0:
                window_of(s - 2)
            if turn == 1:
                for load in loads[:4]:
                    load.wait()
            if turn >= 1:
                mix((turn - 1) // 2, (turn - 1) % 2)
            if turn >= 2:
                image_of(turn % 2)
    window_of(NSUB - 2)
    send_halo(NSUB - 2)
    mix(NSUB - 1, 1)
    image_of(0)
    image_of(1)
    window_of(NSUB - 1)
    send_halo(NSUB - 1)
    sum_halo(0)
    sum_halo(1)

    for load in loads[4:]:
        load.wait()
    tiles = cells.shape[1] // VTILE

    @pl.loop(0, tiles)
    def _(t):
        at = pl.ds(pl.multiple_of(t * VTILE, VTILE), VTILE)
        for r in range(2):
            laid, block = turned(rows[:, at].astype(F32), cells[0:1, at], r)
            across = iota((SUB // 16, 8, VTILE), 0)
            weights = jnp.where(across == block[None], laid[None], 0.0)
            spread[256 * r : 256 * r + 256, at] = weights.reshape(SUB // 2, VTILE).astype(BF)
            laid, block = turned(cols[:, at], cells[1:2, at], r)
            taps[r, :, at] = laid
            blocks[r, :, at] = block

    sum_halo(2)
    sum_halo(3)
    for s in range(NSUB):
        wait_for(plane_sems.at[s], plane.at[s, 0:15])
    for k in (3, 4, 1, 2, 5, 6, 0):
        peer = last_to[k]
        outbox[k] = plane[readers_ref[peer[0] * 16 + peer[1]]]
        last_copy(k, mine).start()
    fin[mine] = plane[readers_ref[fx * 16 + fy]]
    for k in range(7):
        last_copy(k, last_peer(k + 1, -1)[1]).wait_recv()

    for i in range(4):
        for j in range(16):
            low, high = (fin[place_of(h, j)].astype(F32) for h in (i, i + 4))
            at = (slice(32 * j, 32 * j + 32), slice(128 * i, 128 * i + 128))
            lhs[0, at[0], at[1]] = (low + high).astype(BF)
            lhs[1, at[0], at[1]] = (low - high).astype(BF)
    for r in range(2):
        for p in range(2):
            part = et[r, :, 256 * p : 256 * p + 256]
            done = jnp.dot(lhs[r], part, preferred_element_type=F32)
            low, high = done[:256], done[256:]
            at = (slice(256 * p, 256 * p + 256), slice(256 * r, 256 * r + 256))
            yy[0, at[0], at[1]] = (low + high).astype(BF)
            yy[1, at[0], at[1]] = (low - high).astype(BF)
    for r in range(2):
        grid_t[r] = jnp.dot(en[r], yy[r], preferred_element_type=F32).astype(BF)

    @pl.loop(0, tiles)
    def _(t):
        at = pl.ds(pl.multiple_of(t * VTILE, VTILE), VTILE)
        totals = [0.0, 0.0]
        for r in range(2):
            block = blocks[r, :, at]
            here = iota((SUB // 16, 8, VTILE), 0) == block[None]
            values = jnp.dot(grid_t[r], spread[:, at], preferred_element_type=F32)
            values = values.reshape(2, SUB // 16, 8, VTILE)
            for p in range(2):
                picked = jnp.sum(jnp.where(here, values[p], 0.0), axis=0)
                totals[p] = totals[p] + picked * taps[r, :, at]
        for p in range(2):
            out_ref[p : p + 1, at] = jnp.sum(totals[p], axis=0, keepdims=True)

    wait_for(send_sems.at[0], halo)
    wait_for(send_sems.at[1], plane.at[:, 0:15])
    wait_for(send_sems.at[2], outbox)


def local(sky, sub_off, readers, vis_cells, row_kernel, col_kernel):
    hbm = pl.BlockSpec(memory_space=pltpu.HBM)
    smem = pl.BlockSpec(memory_space=pltpu.SMEM)
    count = vis_cells.shape[1]
    return pl.pallas_call(
        kernel,
        out_shape=jax.ShapeDtypeStruct((2, count), F32),
        in_specs=[hbm, smem, smem] + [hbm] * 9,
        out_specs=pl.BlockSpec(memory_space=pltpu.VMEM),
        scratch_shapes=[
            pltpu.VMEM((2 * FR, FACET), BF),
            pltpu.VMEM((FACET, 2 * K), BF),
            pltpu.VMEM((FACET, 2 * K), BF),
            pltpu.VMEM((2, FR, 2 * K), F32),
            pltpu.VMEM((NSUB, 2, 64, K), F32),
            pltpu.VMEM((NSUB, 2, 64, K), F32),
            pltpu.VMEM((2, K, 2 * K), BF),
            pltpu.VMEM((K, 4 * K), BF),
            pltpu.VMEM((NSUB, 12, 32, 128), BF),
            pltpu.VMEM((NSUB, 11, 32, 128), BF),
            pltpu.VMEM((NSUB, 16, 32, 128), BF),
            pltpu.VMEM((7, 16, 32, 128), BF),
            pltpu.VMEM((8, 16, 32, 128), BF),
            pltpu.VMEM((2, SUB, SUB), BF),
            pltpu.VMEM((2, SUB, SUB), BF),
            pltpu.VMEM((2, SUB, SUB), BF),
            pltpu.VMEM((SUB, count), BF),
            pltpu.VMEM((2, 8, count), F32),
            pltpu.VMEM((2, 8, count), jnp.int32),
            pltpu.VMEM((2, SUB, SUB), BF),
            pltpu.VMEM((2, SUB, SUB), BF),
            pltpu.VMEM((2 * K, 2 * K), BF),
            pltpu.VMEM((4 * K, 384), BF),
            pltpu.VMEM((K, FR), F32),
            pltpu.VMEM((K, FR), F32),
            pltpu.VMEM((2, count), jnp.int32),
            pltpu.VMEM((8, count), BF),
            pltpu.VMEM((8, count), F32),
            pltpu.SemaphoreType.DMA((CHUNKS,)),
            pltpu.SemaphoreType.DMA((9,)),
            pltpu.SemaphoreType.DMA((3,)),
            pltpu.SemaphoreType.DMA((NSUB,)),
            pltpu.SemaphoreType.DMA((NSUB,)),
            pltpu.SemaphoreType.DMA((7,)),
        ],
        compiler_params=pltpu.CompilerParams(
            collective_id=0, has_side_effects=True, vmem_limit_bytes=56 * 2**20
        ),
    )(sky, sub_off, readers, vis_cells, row_kernel, col_kernel, *small_tables(), *grid_tables())


def solution(mesh):
    return jax.shard_map(
        local,
        mesh=mesh,
        in_specs=(
            P("fx", "fy"),
            P(),
            P(),
            P(None, ("fx", "fy")),
            P(None, ("fx", "fy")),
            P(None, ("fx", "fy")),
        ),
        out_specs=P(None, ("fx", "fy")),
        check_vma=False,
    )
```

```python
import math

import jax
import jax.numpy as jnp
import numpy as np
from jax import lax
from jax.experimental import pallas as pl
from jax.experimental.pallas import tpu as pltpu
from jax.sharding import PartitionSpec as P

FACET = 4096
SUB = 512
K = 128
W = 8
FR = 512
NSUB = 4
SKY = 65536
CHUNK = 256
CHUNKS = 2 * FR // CHUNK
VTILE = 256
BF = jnp.bfloat16
F32 = jnp.float32
MESH = pl.DeviceIdType.MESH


def wave(rows, cols, period):
    turn = (np.arange(rows)[:, None] * np.arange(cols)[None, :]) % period
    angle = turn * (2.0 * math.pi / period)
    return np.cos(angle), np.sin(angle)


def small_tables():
    re, im = wave(K, K, K)
    re, im = re / K, -im / K
    cols = np.block([[re.T, im.T], [-im.T, re.T]])
    rows = np.zeros((2, 2, K, 3, 2, 64))
    for f in range(2):
        for t in range(K):
            at, cell = divmod(32 * f + t, 64)
            rows[f, 0, :, at, 0, cell] = re[t]
            rows[f, 1, :, at, 0, cell] = -im[t]
            rows[f, 0, :, at, 1, cell] = im[t]
            rows[f, 1, :, at, 1, cell] = re[t]
    qre, qim = wave(K, FR, SKY // 4)
    scale = 1.0 / math.sqrt(FR)
    return (
        jnp.asarray(cols, BF),
        jnp.asarray(rows.reshape(4 * K, 384), BF),
        jnp.asarray(qre * scale, F32),
        jnp.asarray(-qim * scale, F32),
    )


def grid_tables():
    half = SUB // 2
    re, im = wave(SUB, half, SUB)
    et, en = [], []
    for r in range(2):
        a, b = re[r::2], im[r::2]
        rows = np.stack([np.concatenate([a.T, b.T], 1), np.concatenate([-b.T, a.T], 1)])
        et.append(rows.reshape(2, 4, 64, SUB).transpose(1, 0, 2, 3).reshape(SUB, SUB))
        en.append(np.block([[a, -b], [b, a]]) / 16.0)
    return jnp.asarray(np.stack(et), BF), jnp.asarray(np.stack(en), BF)


def cis(phase):
    turn = phase & 0xFFFF
    quarter = (turn + 8192) >> 14
    x = (turn - (quarter << 14)).astype(F32) * (2.0 * math.pi / SKY)
    x2 = x * x
    c = 1.0 + x2 * (-0.5 + x2 * (1.0 / 24 + x2 * (-1.0 / 720 + x2 * (1.0 / 40320))))
    s = x * (1.0 + x2 * (-1.0 / 6 + x2 * (1.0 / 120 + x2 * (-1.0 / 5040 + x2 * (1.0 / 362880)))))
    odd = (quarter & 1) == 1
    cos = jnp.where(odd, s, c)
    sin = jnp.where(odd, c, s)
    cos = jnp.where(((quarter + 1) & 2) != 0, -cos, cos)
    sin = jnp.where((quarter & 2) != 0, -sin, sin)
    return cos, sin


def iota(shape, dim):
    return lax.broadcasted_iota(jnp.int32, shape, dim)


def turned(kernel, start, r):
    head = (start + 1 - r) >> 1
    first = head & 7
    even = jnp.concatenate([kernel[e : e + 1] for e in (0, 2, 4, 6)], 0)
    odd = jnp.concatenate([kernel[e : e + 1] for e in (1, 3, 5, 7)], 0)
    taps = jnp.where(((start + r) & 1) == 0, even, odd)
    taps = jnp.concatenate([taps, jnp.zeros_like(taps)], 0)
    laid = taps
    for turn in range(1, 8):
        laid = jnp.where(first == turn, jnp.roll(taps, turn, 0), laid)
    return laid, (head >> 3) + jnp.where(iota(taps.shape, 0) < first, 1, 0)


def place_of(i, j):
    j = (j + 15) % 16
    x, y, z, core = 2 * (j // 8) + i % 2, i // 2, (j // 2) % 4, j % 2
    return (4 + z, x * 4 + y) if core else (x, z * 4 + y)


def kernel(
    sky_ref, off_ref, readers_ref, cells_ref, rows_ref, cols_ref,
    dc_ref, dr_ref, qre_ref, qim_ref, et_ref, en_ref, out_ref,
    sky_v, va, vb, acc, coarse, fine, mid, images, pieces, halo, plane, outbox, fin,
    lhs, yy, grid_t, spread, taps, blocks, et, en, dc, dr, qre_v, qim_v, cells, rows, cols,
    sky_sems, load_sems, send_sems, halo_sems, plane_sems, last_sems,
):
    fx, fy = lax.axis_index("fx"), lax.axis_index("fy")
    y, core, z = fx // 2, fy % 2, (fy // 2) % 4
    x = 2 * (fy // 8) + fx % 2
    first = core == 0

    def sky_copy(c):
        part = pl.ds(c * CHUNK, CHUNK)
        return pltpu.make_async_copy(sky_ref.at[part], sky_v.at[part], sky_sems.at[c])

    moves = [
        (dc_ref, dc), (dr_ref, dr), (qre_ref, qre_v), (qim_ref, qim_v),
        (cells_ref, cells), (rows_ref, rows), (cols_ref, cols), (et_ref, et), (en_ref, en),
    ]
    loads = [
        pltpu.make_async_copy(src, dst, load_sems.at[n]) for n, (src, dst) in enumerate(moves)
    ]
    for c in range(CHUNKS):
        sky_copy(c).start()
        if c == CHUNKS // 2 - 1:
            for load in loads[:4]:
                load.start()
    for load in loads[4:]:
        load.start()

    def device(x, y, z, core):
        return (2 * y + x % 2, (x // 2) * 8 + 2 * z + core)

    def axis_of(core):
        return jnp.where(core == 0, x, z)

    def halo_peer(k, sign):
        return ((fx + sign * (k // 4) + 8) % 8, (fy + sign * (k % 4 - 1) + 16) % 16)

    def plane_peer(k, sign):
        far = (jnp.where(first, z, x) + sign * (k // 4) + 4) % 4
        yy = (y + sign * (k % 4) + 4) % 4
        return device(jnp.where(first, x, far), yy, jnp.where(first, far, z), core), far * 4 + yy

    def last_peer(k, sign):
        other = (core + k % 2) % 2
        mover = core if sign == 1 else other
        place = (axis_of(mover) + sign * (k // 2) + 4) % 4
        xx, zz = jnp.where(mover == 0, place, x), jnp.where(mover == 0, z, place)
        slot = mover * 4 + (axis_of(mover) if sign == 1 else place)
        return device(xx, y, zz, other), slot

    halo_ks = [k for k in range(12) if k != 1]
    halo_to = [halo_peer(k, 1) for k in halo_ks]
    plane_to = [plane_peer(k, 1)[0] for k in range(1, 16)]
    last_to = [last_peer(k, 1)[0] for k in range(1, 8)]
    barrier = pltpu.get_barrier_semaphore()
    for k in halo_ks:
        pl.semaphore_signal(barrier, inc=1, device_id=halo_peer(k, -1), device_id_type=MESH)
    for k in range(1, 16):
        pl.semaphore_signal(barrier, inc=1, device_id=plane_peer(k, -1)[0], device_id_type=MESH)
    for k in range(1, 8):
        pl.semaphore_signal(barrier, inc=1, device_id=last_peer(k, -1)[0], device_id_type=MESH)

    own = jnp.where(first, z, x) * 4 + y
    mine = core * 4 + axis_of(core)

    def halo_copy(s, k):
        return pltpu.make_async_remote_copy(
            src_ref=pieces.at[s, k], dst_ref=halo.at[s, k],
            send_sem=send_sems.at[0], recv_sem=halo_sems.at[s],
            device_id=halo_to[k], device_id_type=MESH,
        )

    def plane_copy(s, k):
        return pltpu.make_async_remote_copy(
            src_ref=plane.at[s, own], dst_ref=plane.at[s, own],
            send_sem=send_sems.at[1], recv_sem=plane_sems.at[s],
            device_id=plane_to[k], device_id_type=MESH,
        )

    def last_copy(k, slot):
        return pltpu.make_async_remote_copy(
            src_ref=outbox.at[k], dst_ref=fin.at[slot],
            send_sem=send_sems.at[2], recv_sem=last_sems.at[k],
            device_id=last_to[k], device_id_type=MESH,
        )

    def wait_for(sem, ref):
        pltpu.make_async_copy(ref, ref, sem).wait()

    step, lane = iota((64, K), 0), iota((64, K), 1)
    for s in range(NSUB):
        freq = off_ref[1, s] + 4 * lane
        cos, sin = cis(freq * (64 * step + FACET * fy) + SKY // 4 * lane * fy)
        coarse[s, 0] = cos
        coarse[s, 1] = -sin
        cos, sin = cis(freq * step)
        fine[s, 0] = cos * (1.0 / 64)
        fine[s, 1] = -sin * (1.0 / 64)

    def fill(s, h, ref):
        bre, bim = fine[s, 0], fine[s, 1]
        are, aim = coarse[s, 0, pl.ds(h, 1), :], coarse[s, 1, pl.ds(h, 1), :]
        at = pl.ds(pl.multiple_of(h * 64, 64), 64)
        ref[at, 0:K] = (are * bre - aim * bim).astype(BF)
        ref[at, K : 2 * K] = (are * bim + aim * bre).astype(BF)

    def mix(s, f):
        cos, sin = cis(off_ref[0, s] * (FACET * (2 * fx + f) + iota((1, FR), 1)))
        qre, qim = qre_v[...], qim_v[...]
        ure, uim = qre * cos + qim * sin, qim * cos - qre * sin
        if f == 1:
            sign = jnp.where((iota((K, 1), 0) & 1) == 1, -1.0, 1.0)
            ure, uim = ure * sign, uim * sign
        table = jnp.concatenate([ure, uim], 0).astype(BF)
        mixed = jnp.dot(table, acc[f].astype(BF), preferred_element_type=F32)
        mid[f, :, 0:K] = (mixed[:K, :K] - mixed[K:, K:]).astype(BF)
        mid[f, :, K : 2 * K] = (mixed[:K, K:] + mixed[K:, :K]).astype(BF)

    def image_of(f):
        image = jnp.dot(mid[f], dc[...], preferred_element_type=F32)
        images[:, 2 * K * f : 2 * K * f + K] = image[:, :K].T.astype(BF)
        images[:, 2 * K * f + K : 2 * K * f + 2 * K] = image[:, K:].T.astype(BF)

    def window_of(s):
        window = jnp.dot(images[...], dr[...], preferred_element_type=F32).astype(BF)
        for k in range(12):
            di, dj = divmod(k, 4)
            at = halo_ks.index(k) if k in halo_ks else 11
            pieces[s, at] = window[32 * dj : 32 * dj + 32, 128 * di : 128 * di + 128]

    def send_halo(s):
        for k in range(11):
            halo_copy(s, k).start()

    def sum_halo(s):
        wait_for(halo_sems.at[s], halo.at[s])
        total = pieces[s, 11].astype(F32)
        for k in range(11):
            total = total + halo[s, k].astype(F32)
        plane[s, own] = total.astype(BF)
        for k in range(15):
            plane_copy(s, k).start()

    @pl.loop(0, 16)
    def _(h):
        for d in range(4):
            fill(0, 4 * h + d, va)

    for s in range(NSUB):
        table, after = (va, vb) if s % 2 == 0 else (vb, va)
        for f in range(2):
            if s == 0:
                for c in range(CHUNKS // 2):
                    sky_copy(f * CHUNKS // 2 + c).wait()
            if 2 * s + f == 7:
                pl.semaphore_wait(barrier, 33)
                send_halo(0)
                send_halo(1)
            rows_of_facet = sky_v[FR * f : FR * f + FR, :]
            acc[f] = jnp.dot(rows_of_facet, table[...], preferred_element_type=F32)
            if s + 1 < NSUB:
                for h in range(32):
                    fill(s + 1, 32 * f + h, after)
            turn = 2 * s + f
            if turn >= 4 and f == 0:
                window_of(s - 2)
            if turn == 1:
                for load in loads[:4]:
                    load.wait()
            if turn >= 1:
                mix((turn - 1) // 2, (turn - 1) % 2)
            if turn >= 2:
                image_of(turn % 2)
    window_of(NSUB - 2)
    send_halo(NSUB - 2)
    mix(NSUB - 1, 1)
    image_of(0)
    image_of(1)
    window_of(NSUB - 1)
    send_halo(NSUB - 1)

    for load in loads[4:]:
        load.wait()
    tiles = cells.shape[1] // VTILE

    @pl.loop(0, tiles)
    def _(t):
        at = pl.ds(pl.multiple_of(t * VTILE, VTILE), VTILE)
        for r in range(2):
            laid, block = turned(rows[:, at].astype(F32), cells[0:1, at], r)
            across = iota((SUB // 16, 8, VTILE), 0)
            weights = jnp.where(across == block[None], laid[None], 0.0)
            spread[256 * r : 256 * r + 256, at] = weights.reshape(SUB // 2, VTILE).astype(BF)
            laid, block = turned(cols[:, at], cells[1:2, at], r)
            taps[r, :, at] = laid
            blocks[r, :, at] = block

    for s in range(NSUB):
        sum_halo(s)
    for s in range(NSUB):
        wait_for(plane_sems.at[s], plane.at[s, 0:15])
    for k in (3, 4, 1, 2, 5, 6, 0):
        peer = last_to[k]
        outbox[k] = plane[readers_ref[peer[0] * 16 + peer[1]]]
        last_copy(k, mine).start()
    fin[mine] = plane[readers_ref[fx * 16 + fy]]
    for k in range(7):
        last_copy(k, last_peer(k + 1, -1)[1]).wait_recv()

    for i in range(4):
        for j in range(16):
            low, high = (fin[place_of(h, j)].astype(F32) for h in (i, i + 4))
            at = (slice(32 * j, 32 * j + 32), slice(128 * i, 128 * i + 128))
            lhs[0, at[0], at[1]] = (low + high).astype(BF)
            lhs[1, at[0], at[1]] = (low - high).astype(BF)
    for r in range(2):
        for p in range(2):
            part = et[r, :, 256 * p : 256 * p + 256]
            done = jnp.dot(lhs[r], part, preferred_element_type=F32)
            low, high = done[:256], done[256:]
            at = (slice(256 * p, 256 * p + 256), slice(256 * r, 256 * r + 256))
            yy[0, at[0], at[1]] = (low + high).astype(BF)
            yy[1, at[0], at[1]] = (low - high).astype(BF)
    for r in range(2):
        grid_t[r] = jnp.dot(en[r], yy[r], preferred_element_type=F32).astype(BF)

    @pl.loop(0, tiles, unroll=4)
    def _(t):
        at = pl.ds(pl.multiple_of(t * VTILE, VTILE), VTILE)
        totals = [0.0, 0.0]
        for r in range(2):
            block = blocks[r, :, at]
            here = iota((SUB // 16, 8, VTILE), 0) == block[None]
            values = jnp.dot(grid_t[r], spread[:, at], preferred_element_type=F32)
            values = values.reshape(2, SUB // 16, 8, VTILE)
            for p in range(2):
                picked = jnp.sum(jnp.where(here, values[p], 0.0), axis=0)
                totals[p] = totals[p] + picked * taps[r, :, at]
        for p in range(2):
            out_ref[p : p + 1, at] = jnp.sum(totals[p], axis=0, keepdims=True)

    wait_for(send_sems.at[0], halo)
    wait_for(send_sems.at[1], plane.at[:, 0:15])
    wait_for(send_sems.at[2], outbox)


def local(sky, sub_off, readers, vis_cells, row_kernel, col_kernel):
    hbm = pl.BlockSpec(memory_space=pltpu.HBM)
    smem = pl.BlockSpec(memory_space=pltpu.SMEM)
    count = vis_cells.shape[1]
    return pl.pallas_call(
        kernel,
        out_shape=jax.ShapeDtypeStruct((2, count), F32),
        in_specs=[hbm, smem, smem] + [hbm] * 9,
        out_specs=pl.BlockSpec(memory_space=pltpu.VMEM),
        scratch_shapes=[
            pltpu.VMEM((2 * FR, FACET), BF),
            pltpu.VMEM((FACET, 2 * K), BF),
            pltpu.VMEM((FACET, 2 * K), BF),
            pltpu.VMEM((2, FR, 2 * K), F32),
            pltpu.VMEM((NSUB, 2, 64, K), F32),
            pltpu.VMEM((NSUB, 2, 64, K), F32),
            pltpu.VMEM((2, K, 2 * K), BF),
            pltpu.VMEM((K, 4 * K), BF),
            pltpu.VMEM((NSUB, 12, 32, 128), BF),
            pltpu.VMEM((NSUB, 11, 32, 128), BF),
            pltpu.VMEM((NSUB, 16, 32, 128), BF),
            pltpu.VMEM((7, 16, 32, 128), BF),
            pltpu.VMEM((8, 16, 32, 128), BF),
            pltpu.VMEM((2, SUB, SUB), BF),
            pltpu.VMEM((2, SUB, SUB), BF),
            pltpu.VMEM((2, SUB, SUB), BF),
            pltpu.VMEM((SUB, count), BF),
            pltpu.VMEM((2, 8, count), F32),
            pltpu.VMEM((2, 8, count), jnp.int32),
            pltpu.VMEM((2, SUB, SUB), BF),
            pltpu.VMEM((2, SUB, SUB), BF),
            pltpu.VMEM((2 * K, 2 * K), BF),
            pltpu.VMEM((4 * K, 384), BF),
            pltpu.VMEM((K, FR), F32),
            pltpu.VMEM((K, FR), F32),
            pltpu.VMEM((2, count), jnp.int32),
            pltpu.VMEM((8, count), BF),
            pltpu.VMEM((8, count), F32),
            pltpu.SemaphoreType.DMA((CHUNKS,)),
            pltpu.SemaphoreType.DMA((9,)),
            pltpu.SemaphoreType.DMA((3,)),
            pltpu.SemaphoreType.DMA((NSUB,)),
            pltpu.SemaphoreType.DMA((NSUB,)),
            pltpu.SemaphoreType.DMA((7,)),
        ],
        compiler_params=pltpu.CompilerParams(
            collective_id=0, has_side_effects=True, vmem_limit_bytes=56 * 2**20
        ),
    )(sky, sub_off, readers, vis_cells, row_kernel, col_kernel, *small_tables(), *grid_tables())


def solution(mesh):
    return jax.shard_map(
        local,
        mesh=mesh,
        in_specs=(
            P("fx", "fy"),
            P(),
            P(),
            P(None, ("fx", "fy")),
            P(None, ("fx", "fy")),
            P(None, ("fx", "fy")),
        ),
        out_specs=P(None, ("fx", "fy")),
        check_vma=False,
    )
```
